128 devices in a mesh: dp: 16 (over z, x), tensor: 8 (over y, core).
Axes of the slice: x: 4, y: 4, z: 4, core: 2. Of those that a mesh axis runs over, the one named last changes fastest.
Arguments:
- tokens: bfloat16 [8192, 1024], P('dp'), may hold values from -6 to 6
- segments: int32 [8192], replicated, may hold values from 0 to 11, as said below
- attn_gain: bfloat16 [1024], replicated, may hold values from 0.099609375 to 1.8984375
- query_weight: bfloat16 [1024, 1024], P(None, 'tensor'), may hold values from -0.1875 to 0.1875
- key_weight: bfloat16 [1024, 512], P(None, 'tensor'), may hold values from -0.1875 to 0.1875
- value_weight: bfloat16 [1024, 512], P(None, 'tensor'), may hold values from -0.1875 to 0.1875
- query_gain: bfloat16 [64], replicated, may hold values from 0.099609375 to 1.8984375
- key_gain: bfloat16 [64], replicated, may hold values from 0.099609375 to 1.8984375
- out_weight: bfloat16 [1024, 1024], P('tensor'), may hold values from -4 to 4
- ffn_gain: bfloat16 [1024], replicated, may hold values from 0.099609375 to 1.8984375
- gate_weight: bfloat16 [1024, 4608], P(None, 'tensor'), may hold values from -0.1875 to 0.1875
- up_weight: bfloat16 [1024, 4608], P(None, 'tensor'), may hold values from -0.1875 to 0.1875
- down_weight: bfloat16 [4608, 1024], P('tensor'), may hold values from -0.09375 to 0.09375
- cotangent: bfloat16 [8192, 1024], P('dp'), may hold values from -6 to 6
Outputs:
- block_output: bfloat16 [8192, 1024], P(('dp', 'tensor'))
- input_grad: float32 [8192, 1024], P(('dp', 'tensor'))
- attn_gain_grad: float32 [1024], P('dp')
- query_weight_grad: float32 [1024, 1024], P('dp', 'tensor')
- key_weight_grad: float32 [1024, 512], P('dp', 'tensor')
- value_weight_grad: float32 [1024, 512], P('dp', 'tensor')
- query_gain_grad: float32 [64], P('dp')
- key_gain_grad: float32 [64], P('dp')
- out_weight_grad: float32 [1024, 1024], P('tensor', 'dp')
- ffn_gain_grad: float32 [1024], P('dp')
- gate_weight_grad: float32 [1024, 4608], P('dp', 'tensor')
- up_weight_grad: float32 [1024, 4608], P('dp', 'tensor')
- down_weight_grad: float32 [4608, 1024], P('tensor', 'dp')
The draws below stay inside these ranges and needn't reach their ends.
Inputs may be any that keep to these rules, and one draw needn't show every extreme that they name: `segments`: each aligned sequence of 2048 tokens holds exactly three documents, numbered on from those of the sequence before, never falling; its first and its last document hold at least 204 tokens and fewer than 512.
All inputs are finite; a program needn't handle non-finite values.
Results may differ from the reference program's by a relative error of at most 0.038.
Values may be sent and summed in bfloat16 or wider, within the bound.
No kernel may reach another device: no remote copies, remote signals or barrier semaphores. Data moves between devices by JAX's collectives and lax.ppermute only.
A program may use at most 128 MiB of HBM per device.

```python
import jax
import jax.numpy as jnp
from jax import lax

D = 1024
H = 16
KVH = 8
HD = 64
FF = 4608
SEQ_LEN = 2048
TOK_DEV = 512
TOKENS = 8192


def draw_segments(key, part):
    key = jax.random.fold_in(key, 17)
    first_key, last_key = jax.random.split(key, 2)
    seq_count = TOKENS // SEQ_LEN
    lowest = SEQ_LEN // 10
    highest = min(TOK_DEV, lowest + SEQ_LEN // 8)
    first_len = jax.random.randint(first_key, (seq_count,), lowest, highest)
    last_len = jax.random.randint(last_key, (seq_count,), lowest, highest)
    places = jnp.arange(TOKENS, dtype=jnp.int32)
    seq_of = places // SEQ_LEN
    within = places - seq_of * SEQ_LEN
    first_here = jnp.take(first_len, seq_of)
    last_here = jnp.take(last_len, seq_of)
    second = (within >= first_here).astype(jnp.int32)
    third = (within >= SEQ_LEN - last_here).astype(jnp.int32)
    return (3 * seq_of + second + third).astype(jnp.int32)


def level_of(key, shape, cuts, least, top_value):
    factor_of, own = 1.0, jax.random.fold_in(key, 6)
    for dim, blocks in cuts:
        draws = jnp.exp(jax.random.uniform(jax.random.fold_in(own, dim), (blocks,), jnp.float32, least / len(cuts), top_value / len(cuts)))
        factor_of = factor_of * jnp.repeat(draws, shape[dim] // blocks).reshape([-1 if axis == dim else 1 for axis in range(len(shape))])
    return factor_of


def centred(own_key, dims, width, limit, cuts=(), kind=jnp.bfloat16):
    loudness = level_of(own_key, dims, cuts, -0.22, 0.18) if cuts else 1.0
    entries = jax.random.normal(own_key, dims, jnp.float32) * width * loudness
    return jnp.minimum(jnp.maximum(entries, -limit), limit).astype(kind)


def setup_inputs(seed: int = 0) -> dict:
    seeds = jax.random.split(jax.random.key(seed), 15)
    return {
        "tokens": centred(seeds[0], (TOKENS, D), 1.0, 6.0, ((0, 16),)),
        "segments": draw_segments(jax.random.fold_in(seeds[14], 71), 0),
        "attn_gain": jnp.clip(1.0 + 0.18 * jax.random.normal(seeds[2], (D,), jnp.float32), 0.099609375, 1.8984375).astype(jnp.bfloat16),
        "query_weight": centred(seeds[3], (D, H * HD), D ** -0.5, 0.1875, ((1, 8),)),
        "key_weight": centred(seeds[4], (D, KVH * HD), D ** -0.5, 0.1875, ((1, 8),)),
        "value_weight": centred(seeds[5], (D, KVH * HD), D ** -0.5, 0.1875, ((1, 8),)),
        "query_gain": jnp.clip(1.0 + 0.18 * jax.random.normal(seeds[6], (HD,), jnp.float32), 0.099609375, 1.8984375).astype(jnp.bfloat16),
        "key_gain": jnp.clip(1.0 + 0.18 * jax.random.normal(seeds[7], (HD,), jnp.float32), 0.099609375, 1.8984375).astype(jnp.bfloat16),
        "out_weight": centred(seeds[8], (H * HD, D), (max(1, 4 * H * HD // SEQ_LEN)) ** -0.5, 4.0, ((0, 8),)),
        "ffn_gain": jnp.clip(1.0 + 0.18 * jax.random.normal(seeds[9], (D,), jnp.float32), 0.099609375, 1.8984375).astype(jnp.bfloat16),
        "gate_weight": centred(seeds[10], (D, FF), D ** -0.5, 0.1875, ((1, 8),)),
        "up_weight": centred(seeds[11], (D, FF), D ** -0.5, 0.1875, ((1, 8),)),
        "down_weight": centred(seeds[12], (FF, D), FF ** -0.5, 0.09375, ((0, 8),)),
        "cotangent": centred(seeds[13], (TOKENS, D), 1.0, 6.0, ((0, 16),)),
    }


EPSILON = 1e-05
ROPE_BASE = 1000000.0
MASKED = -1e+30

@jax.custom_vjp
def low(v):
    return lax.optimization_barrier(v.astype(jnp.bfloat16)).astype(jnp.float32)

@jax.custom_vjp
def low_back(v):
    return v

def low_keep(v):
    return (low(v), None)

def low_pass(kept, grad):
    return (grad,)

def back_keep(v):
    return (v, None)

def back_low(kept, grad):
    return (low(grad),)
low.defvjp(low_keep, low_pass)
low_back.defvjp(back_keep, back_low)

def matmul(left, right):
    return jnp.dot(left, right, precision=lax.Precision.HIGHEST)

def rms_scale(array_in, norm_gain):
    inverse = lax.rsqrt(lax.optimization_barrier(jnp.mean(array_in * array_in, axis=-1, keepdims=True)) + EPSILON)
    return array_in * inverse * norm_gain

def rotate(array_in, cosine_table, sine_table):
    half_dim = array_in.shape[-1] // 2
    former = array_in[..., :half_dim]
    latter = array_in[..., half_dim:]
    return jnp.concatenate([former * cosine_table - latter * sine_table, latter * cosine_table + former * sine_table], axis=-1)

def forward(tokens, segments, attn_gain, query_weight, key_weight, value_weight, query_gain, key_gain, out_weight, ffn_gain, gate_weight, up_weight, down_weight):
    total_rows = tokens.shape[0]
    group_size = H // KVH
    score_scale = HD ** (-0.5)
    places = jnp.arange(total_rows, dtype=jnp.int32)
    seq_places = places % SEQ_LEN
    frequency = ROPE_BASE ** (-jnp.arange(HD // 2, dtype=jnp.float32) * 2.0 / HD)
    angles = seq_places.astype(jnp.float32)[:, None] * frequency[None, :]
    cosine_table = jnp.cos(angles)[:, None, :]
    sine_table = jnp.sin(angles)[:, None, :]
    normed = low(rms_scale(tokens, attn_gain))
    query_raw = low_back(matmul(normed, query_weight)).reshape(total_rows, H, HD)
    key_raw = low_back(matmul(normed, key_weight)).reshape(total_rows, KVH, HD)
    values = low(low_back(matmul(normed, value_weight))).reshape(total_rows, KVH, HD)
    queries = low(rotate(rms_scale(query_raw, query_gain), cosine_table, sine_table))
    keys = low(rotate(rms_scale(key_raw, key_gain), cosine_table, sine_table))
    block_rows = min(512, SEQ_LEN)
    block_count = total_rows // block_rows
    query_blocks = queries.reshape(block_count, block_rows, KVH, group_size, HD)
    block_ids = jnp.arange(block_count, dtype=jnp.int32)

    def attend(pieces):
        query_part, block_id = pieces
        first_row = block_id * block_rows
        seq_begin = first_row // SEQ_LEN * SEQ_LEN
        key_part = lax.dynamic_slice_in_dim(keys, seq_begin, SEQ_LEN)
        value_part = lax.dynamic_slice_in_dim(values, seq_begin, SEQ_LEN)
        key_segs = lax.dynamic_slice_in_dim(segments, seq_begin, SEQ_LEN)
        query_segs = lax.dynamic_slice_in_dim(segments, first_row, block_rows)
        key_places = seq_begin + jnp.arange(SEQ_LEN, dtype=jnp.int32)
        query_places = first_row + jnp.arange(block_rows, dtype=jnp.int32)
        scores = low_back(jnp.einsum('qkgd,tkd->kgqt', query_part, key_part, precision=lax.Precision.HIGHEST)) * score_scale
        allowed = (query_segs[:, None] == key_segs[None, :]) & (key_places[None, :] <= query_places[:, None])
        scores = jnp.where(allowed[None, None], scores, MASKED)
        row_peak = lax.optimization_barrier(jnp.max(scores, axis=-1, keepdims=True))
        weights = jnp.exp(scores - row_peak)
        softmax_low = low(weights / lax.optimization_barrier(jnp.sum(weights, axis=-1, keepdims=True)))
        return jnp.einsum('kgqt,tkd->qkgd', softmax_low, value_part, precision=lax.Precision.HIGHEST)
    outputs = lax.map(jax.checkpoint(attend), (query_blocks, block_ids))
    attended = low(low_back(outputs.reshape(total_rows, H * HD)))
    branch = low_back(matmul(attended, out_weight))
    hidden = tokens + branch
    normed_ffn = low(rms_scale(hidden, ffn_gain))
    gate_pre = low_back(matmul(normed_ffn, gate_weight))
    upward = low_back(matmul(normed_ffn, up_weight))
    active = low(jax.nn.silu(gate_pre) * upward)
    return hidden + matmul(active, down_weight)

def reference(tokens, segments, attn_gain, query_weight, key_weight, value_weight, query_gain, key_gain, out_weight, ffn_gain, gate_weight, up_weight, down_weight, cotangent):
    floats = [array_in.astype(jnp.float32) for array_in in (tokens, attn_gain, query_weight, key_weight, value_weight, query_gain, key_gain, out_weight, ffn_gain, gate_weight, up_weight, down_weight)]

    def wrapped(*arrays):
        return forward(arrays[0], segments, *arrays[1:])
    result, pullback = jax.vjp(wrapped, *floats)
    gradients = pullback(cotangent.astype(jnp.float32))
    return (result.astype(jnp.bfloat16), gradients[0], gradients[1], gradients[2], gradients[3], gradients[4], gradients[5], gradients[6], gradients[7], gradients[8], gradients[9], gradients[10], gradients[11])
```

```python
import jax
import jax.numpy as jnp
from jax import lax
from jax.sharding import PartitionSpec as P

SEQ_LEN = 2048


EPSILON = 1e-05
ROPE_BASE = 1000000.0
MASKED = -1e30


X_SIZE = 4
Y_SIZE = 4


def in_sequence(value, steps):
    count = lax.axis_size("dp")
    pairs = [
        (source, source + steps)
        for source in range(count)
        if 0 <= source + steps < count and (source + steps) // X_SIZE == source // X_SIZE
    ]
    return lax.ppermute(value, "dp", pairs)


def over_cores(value):
    count = lax.axis_size("tensor")
    return lax.ppermute(value, "tensor", [(i, i ^ 1) for i in range(count)])


def along_y(value, steps):
    count = lax.axis_size("tensor")
    pairs = [(i, ((i // 2 + steps) % Y_SIZE) * 2 + i % 2) for i in range(count)]
    return lax.ppermute(value, "tensor", pairs)


def gather_relative(value):
    mine = jnp.stack([value] + [along_y(value, k) for k in range(1, Y_SIZE)])
    return mine, over_cores(mine)


def gather_rows(value):
    rows = value.shape[0]
    mine, other = gather_relative(value)
    y, core = lax.axis_index("tensor") // 2, lax.axis_index("tensor") % 2
    first = jnp.where(core == 0, mine, other)
    second = jnp.where(core == 0, other, mine)
    both = jnp.stack([first, second], axis=1)[::-1]
    twice = jnp.concatenate([both, both], axis=0)
    ordered = lax.dynamic_slice_in_dim(twice, (Y_SIZE - 1 - y) % Y_SIZE, Y_SIZE, axis=0)
    return ordered.reshape(2 * Y_SIZE * rows, -1)


def sum_rows_at_owner(value, extra=None):
    y, core = lax.axis_index("tensor") // 2, lax.axis_index("tensor") % 2
    halves = value.reshape(Y_SIZE, 2, -1, value.shape[1])
    if extra is not None:
        extra = jnp.broadcast_to(extra[None, None], (Y_SIZE, 2, *extra.shape))
        halves = jnp.concatenate([halves, extra], axis=2)
    keep = lax.dynamic_index_in_dim(halves, core, 1, keepdims=False)
    give = lax.dynamic_index_in_dim(halves, 1 - core, 1, keepdims=False)
    got = over_cores(give)
    total = (keep.astype(jnp.float32) + got.astype(jnp.float32)).astype(jnp.bfloat16)
    share = [
        lax.dynamic_index_in_dim(total, (y + k) % Y_SIZE, 0, keepdims=False) for k in range(Y_SIZE)
    ]
    out = share[0].astype(jnp.float32)
    for k in (1, 3, 2):
        out = out + along_y(share[k], k).astype(jnp.float32)
    return out


def sum_over_dp(value):
    devices = lax.axis_size("dp")
    parts = value.reshape(devices, -1, value.shape[1])
    arrived = lax.all_to_all(parts, "dp", split_axis=0, concat_axis=0, tiled=True)
    return arrived.astype(jnp.float32).sum(axis=0)


def rotate(array_in, cosine_table, sine_table):
    half_dim = array_in.shape[-1] // 2
    former = array_in[..., :half_dim]
    latter = array_in[..., half_dim:]
    return jnp.concatenate(
        [former * cosine_table - latter * sine_table, latter * cosine_table + former * sine_table],
        axis=-1,
    )


def rotate_back(array_in, cosine_table, sine_table):
    half_dim = array_in.shape[-1] // 2
    former = array_in[..., :half_dim]
    latter = array_in[..., half_dim:]
    return jnp.concatenate(
        [former * cosine_table + latter * sine_table, latter * cosine_table - former * sine_table],
        axis=-1,
    )


def norm_forward(array_in, norm_gain):
    inverse = lax.rsqrt(jnp.mean(array_in * array_in, axis=-1, keepdims=True) + EPSILON)
    unit_part = array_in * inverse
    return (unit_part, inverse, unit_part * norm_gain)


def norm_backward(grad_result, unit_part, inverse, norm_gain):
    grad_unit = grad_result * norm_gain
    return inverse * (
        grad_unit - unit_part * jnp.mean(grad_unit * unit_part, axis=-1, keepdims=True)
    )


def local(
    tokens,
    segments,
    attn_gain,
    query_weight,
    key_weight,
    value_weight,
    query_gain,
    key_gain,
    out_weight,
    ffn_gain,
    gate_weight,
    up_weight,
    down_weight,
    cotangent,
):
    tok_rows = tokens.shape[0]
    head_dim = query_gain.shape[0]
    local_heads = query_weight.shape[1] // head_dim
    local_groups = key_weight.shape[1] // head_dim
    group_size = local_heads // local_groups
    key_width = local_groups * head_dim
    context = SEQ_LEN // tok_rows
    seen_keys = context * tok_rows
    share_rows = tok_rows // lax.axis_size("tensor")
    share_start = lax.axis_index("tensor") * share_rows
    score_scale = head_dim ** (-0.5)
    offset = lax.axis_index("dp") * tok_rows
    seq_start = offset // SEQ_LEN * SEQ_LEN
    row_ids = jnp.arange(tok_rows, dtype=jnp.int32)
    places = offset + row_ids
    own_segments = lax.dynamic_slice_in_dim(segments, offset, tok_rows)
    frequency = ROPE_BASE ** (-jnp.arange(head_dim // 2, dtype=jnp.float32) * 2.0 / head_dim)
    angles = (places - seq_start).astype(jnp.float32)[:, None] * frequency[None, :]
    cosine_table = jnp.cos(angles)[:, None, :]
    sine_table = jnp.sin(angles)[:, None, :]
    attn_scale = attn_gain.astype(jnp.float32)
    ffn_scale = ffn_gain.astype(jnp.float32)
    query_scale = query_gain.astype(jnp.float32)
    key_scale = key_gain.astype(jnp.float32)

    def share_of(array_in):
        return lax.dynamic_slice_in_dim(array_in, share_start, share_rows)

    place_pieces = []
    segment_pieces = []
    for shift_by in range(context):
        piece_start = offset - shift_by * tok_rows
        piece_places = piece_start + row_ids
        piece_segments = lax.dynamic_slice_in_dim(segments, jnp.maximum(piece_start, 0), tok_rows)
        segment_pieces.append(jnp.where(piece_places >= seq_start, piece_segments, -1))
        place_pieces.append(piece_places)
    key_places = jnp.concatenate(place_pieces, axis=0)
    key_segments = jnp.concatenate(segment_pieces, axis=0)
    inputs = tokens.astype(jnp.float32)
    unit_one, inverse_one, normed = norm_forward(inputs, attn_scale)
    normed_low = normed.astype(jnp.bfloat16)
    query_raw = jnp.dot(normed_low, query_weight, preferred_element_type=jnp.float32).reshape(
        tok_rows, local_heads, head_dim
    )
    key_raw = jnp.dot(normed_low, key_weight, preferred_element_type=jnp.float32).reshape(
        tok_rows, local_groups, head_dim
    )
    value_low = jnp.dot(normed_low, value_weight, preferred_element_type=jnp.float32).astype(
        jnp.bfloat16
    )
    query_unit, query_inverse, query_normed = norm_forward(query_raw, query_scale)
    query_low = rotate(query_normed, cosine_table, sine_table).astype(jnp.bfloat16)
    key_unit, key_inverse, key_normed = norm_forward(key_raw, key_scale)
    key_low = rotate(key_normed, cosine_table, sine_table).astype(jnp.bfloat16)
    packed = jnp.concatenate([key_low.reshape(tok_rows, key_width), value_low], axis=1)
    kv_pieces = [packed]
    for shift_by in range(1, context):
        kv_pieces.append(in_sequence(packed, shift_by))
    gathered = jnp.concatenate(kv_pieces, axis=0)
    all_keys = gathered[:, :key_width].reshape(seen_keys, local_groups, head_dim)
    all_values = gathered[:, key_width:].reshape(seen_keys, local_groups, head_dim)
    block_rows = min(512, tok_rows)
    block_count = tok_rows // block_rows
    query_blocks = query_low.reshape(block_count, block_rows, local_groups, group_size, head_dim)
    place_blocks = places.reshape(block_count, block_rows)
    segment_blocks = own_segments.reshape(block_count, block_rows)

    def masked_scores(query_part, place_part, segment_part):
        scores = (
            jnp.einsum("qkgd,tkd->kgqt", query_part, all_keys, preferred_element_type=jnp.float32)
            * score_scale
        )
        allowed = (segment_part[:, None] == key_segments[None, :]) & (
            key_places[None, :] <= place_part[:, None]
        )
        return jnp.where(allowed[None, None], scores, MASKED)

    def attend(pieces):
        query_part, place_part, segment_part = pieces
        scores = masked_scores(query_part, place_part, segment_part)
        row_peak = jnp.max(scores, axis=-1, keepdims=True)
        weights = jnp.exp(scores - row_peak)
        totals = jnp.sum(weights, axis=-1, keepdims=True)
        probs_low = (weights / totals).astype(jnp.bfloat16)
        output = jnp.einsum(
            "kgqt,tkd->qkgd", probs_low, all_values, preferred_element_type=jnp.float32
        )
        log_total = (row_peak + jnp.log(totals))[..., 0]
        return (output, log_total)

    outputs, log_totals = lax.map(attend, (query_blocks, place_blocks, segment_blocks))
    attended_low = outputs.reshape(tok_rows, local_heads * head_dim).astype(jnp.bfloat16)
    out_mine, out_other = gather_relative(out_weight)
    att_mine, att_other = gather_relative(attended_low)
    att_all = jnp.concatenate(
        [att_mine[k] for k in range(Y_SIZE)] + [att_other[k] for k in range(Y_SIZE)], axis=1
    )
    out_all = jnp.concatenate([out_mine, out_other], axis=0).reshape(-1, out_weight.shape[1])
    hidden = inputs + jnp.dot(att_all, out_all, preferred_element_type=jnp.float32)
    unit_two, inverse_two, normed_two = norm_forward(hidden, ffn_scale)
    normed_two_low = normed_two.astype(jnp.bfloat16)
    gate_pre = jnp.dot(normed_two_low, gate_weight, preferred_element_type=jnp.float32)
    upward = jnp.dot(normed_two_low, up_weight, preferred_element_type=jnp.float32)
    sigmoid_gate = jax.nn.sigmoid(gate_pre)
    silu_gate = gate_pre * sigmoid_gate
    active_low = (silu_gate * upward).astype(jnp.bfloat16)
    ffn_terms = jnp.dot(active_low, down_weight, preferred_element_type=jnp.float32)
    ffn_share = sum_rows_at_owner(ffn_terms.astype(jnp.bfloat16))
    result = (share_of(hidden) + ffn_share).astype(jnp.bfloat16)
    grad_result = cotangent.astype(jnp.float32)
    grad_down_w = jnp.einsum("td,tf->df", cotangent, active_low, preferred_element_type=jnp.float32)
    grad_active = jnp.einsum(
        "td,fd->tf", cotangent, down_weight, preferred_element_type=jnp.float32
    )
    grad_gate = (
        grad_active * upward * sigmoid_gate * (1.0 + gate_pre * (1.0 - sigmoid_gate))
    ).astype(jnp.bfloat16)
    grad_up = (grad_active * silu_gate).astype(jnp.bfloat16)
    grad_gate_w = jnp.einsum(
        "td,tf->df", normed_two_low, grad_gate, preferred_element_type=jnp.float32
    )
    grad_up_w = jnp.einsum("td,tf->df", normed_two_low, grad_up, preferred_element_type=jnp.float32)
    partial_ffn = jnp.einsum(
        "tf,df->td", grad_gate, gate_weight, preferred_element_type=jnp.float32
    ) + jnp.einsum("tf,df->td", grad_up, up_weight, preferred_element_type=jnp.float32)
    grad_normed_share = sum_rows_at_owner(partial_ffn.astype(jnp.bfloat16))
    early = sum_over_dp(
        jnp.concatenate([grad_gate_w, grad_up_w, grad_down_w], axis=1).astype(jnp.bfloat16)
    )
    unit_two_share = share_of(unit_two)
    grad_ffn_gain = jnp.sum(grad_normed_share * unit_two_share, axis=0)
    grad_hidden_share = share_of(grad_result) + norm_backward(
        grad_normed_share, unit_two_share, share_of(inverse_two), ffn_scale
    )
    grad_hidden_low = gather_rows(grad_hidden_share.astype(jnp.bfloat16))
    grad_out_w = jnp.einsum(
        "td,th->dh", grad_hidden_low, attended_low, preferred_element_type=jnp.float32
    )
    grad_attended_low = jnp.einsum(
        "td,hd->th", grad_hidden_low, out_weight, preferred_element_type=jnp.float32
    ).astype(jnp.bfloat16)
    grad_blocks = grad_attended_low.reshape(
        block_count, block_rows, local_groups, group_size, head_dim
    )

    def attend_back(running, pieces):
        key_acc, value_acc = running
        query_part, place_part, segment_part, grad_part, output_part, log_part = pieces
        scores = masked_scores(query_part, place_part, segment_part)
        softmax_full = jnp.exp(scores - log_part[..., None])
        probs_low = softmax_full.astype(jnp.bfloat16)
        grad_probs = jnp.einsum(
            "qkgd,tkd->kgqt", grad_part, all_values, preferred_element_type=jnp.float32
        )
        row_delta = jnp.moveaxis(
            jnp.sum(grad_part.astype(jnp.float32) * output_part, axis=-1), 0, 2
        )[..., None]
        grad_scores = (softmax_full * (grad_probs - row_delta) * score_scale).astype(jnp.bfloat16)
        grad_query = jnp.einsum(
            "kgqt,tkd->qkgd", grad_scores, all_keys, preferred_element_type=jnp.float32
        )
        key_acc = key_acc + jnp.einsum(
            "kgqt,qkgd->tkd", grad_scores, query_part, preferred_element_type=jnp.float32
        )
        value_acc = value_acc + jnp.einsum(
            "kgqt,qkgd->tkd", probs_low, grad_part, preferred_element_type=jnp.float32
        )
        return ((key_acc, value_acc), grad_query)

    empty_grads = jnp.zeros((seen_keys, local_groups, head_dim), jnp.float32)
    (key_acc, value_acc), grad_queries = lax.scan(
        attend_back,
        (empty_grads, empty_grads),
        (query_blocks, place_blocks, segment_blocks, grad_blocks, outputs, log_totals),
    )
    key_terms = jnp.concatenate(
        [key_acc.reshape(seen_keys, key_width), value_acc.reshape(seen_keys, key_width)], axis=1
    )
    local_key_grads = key_terms[:tok_rows]
    for shift_by in range(1, context):
        local_key_grads = local_key_grads + in_sequence(
            key_terms[shift_by * tok_rows : (shift_by + 1) * tok_rows].astype(jnp.bfloat16),
            -shift_by,
        ).astype(jnp.float32)
    grad_key_rot = local_key_grads[:, :key_width].reshape(tok_rows, local_groups, head_dim)
    grad_value_low = local_key_grads[:, key_width:].astype(jnp.bfloat16)
    grad_key_norm = rotate_back(grad_key_rot, cosine_table, sine_table)
    grad_key_gain = jnp.sum(grad_key_norm * key_unit, axis=(0, 1))
    grad_key_low = (
        norm_backward(grad_key_norm, key_unit, key_inverse, key_scale)
        .reshape(tok_rows, key_width)
        .astype(jnp.bfloat16)
    )
    grad_query_norm = rotate_back(
        grad_queries.reshape(tok_rows, local_heads, head_dim), cosine_table, sine_table
    )
    grad_query_gain = jnp.sum(grad_query_norm * query_unit, axis=(0, 1))
    grad_query_low = (
        norm_backward(grad_query_norm, query_unit, query_inverse, query_scale)
        .reshape(tok_rows, local_heads * head_dim)
        .astype(jnp.bfloat16)
    )
    grad_query_w = jnp.einsum(
        "td,th->dh", normed_low, grad_query_low, preferred_element_type=jnp.float32
    )
    grad_key_w = jnp.einsum(
        "td,th->dh", normed_low, grad_key_low, preferred_element_type=jnp.float32
    )
    grad_value_w = jnp.einsum(
        "td,th->dh", normed_low, grad_value_low, preferred_element_type=jnp.float32
    )
    partial_attn = jnp.einsum(
        "th,dh->td", grad_query_low, query_weight, preferred_element_type=jnp.float32
    )
    partial_attn = partial_attn + jnp.einsum(
        "th,dh->td", grad_key_low, key_weight, preferred_element_type=jnp.float32
    )
    partial_attn = partial_attn + jnp.einsum(
        "th,dh->td", grad_value_low, value_weight, preferred_element_type=jnp.float32
    )
    late = sum_over_dp(
        jnp.concatenate([grad_out_w, grad_query_w, grad_key_w, grad_value_w], axis=1).astype(
            jnp.bfloat16
        )
    )
    dp_count = lax.axis_size("dp")
    grad_attn_gain = jnp.sum(partial_attn * unit_one, axis=0)

    def spread(small):
        return jnp.pad(small.reshape(dp_count, -1), ((0, 0), (0, 60))).reshape(1, -1)

    gains = jnp.concatenate(
        [
            grad_attn_gain[None],
            grad_ffn_gain[None],
            spread(grad_query_gain),
            spread(grad_key_gain),
            jnp.zeros((12, grad_attn_gain.shape[0]), jnp.float32),
        ],
        axis=0,
    ).astype(jnp.bfloat16)
    summed = sum_rows_at_owner(partial_attn.astype(jnp.bfloat16), gains)
    grad_normed_share = summed[:share_rows]
    gain_sums = summed[share_rows : share_rows + 4]
    gain_parts = jnp.moveaxis(gain_sums.reshape(4, dp_count, 64), 1, 0).astype(jnp.bfloat16)
    gain_parts = jnp.pad(gain_parts, ((0, 0), (0, 12), (0, 64)))
    gains_here = (
        lax.all_to_all(gain_parts, "dp", split_axis=0, concat_axis=0, tiled=True)
        .astype(jnp.float32)
        .sum(axis=0)
    )
    grad_inputs = grad_hidden_share + norm_backward(
        grad_normed_share, share_of(unit_one), share_of(inverse_one), attn_scale
    )
    hidden_units = gate_weight.shape[1]
    head_width = local_heads * head_dim
    grad_gate_w = early[:, :hidden_units]
    grad_up_w = early[:, hidden_units : 2 * hidden_units]
    grad_down_w = early[:, 2 * hidden_units :].T
    grad_out_w = late[:, :head_width].T
    grad_query_w = late[:, head_width : 2 * head_width]
    grad_key_w = late[:, 2 * head_width : 2 * head_width + key_width]
    grad_value_w = late[:, 2 * head_width + key_width :]
    grad_attn_gain = gains_here[0, :64]
    grad_ffn_gain = gains_here[1, :64]
    grad_query_gain = gains_here[2, :4]
    grad_key_gain = gains_here[3, :4]
    return (
        result,
        grad_inputs,
        grad_attn_gain,
        grad_query_w,
        grad_key_w,
        grad_value_w,
        grad_query_gain,
        grad_key_gain,
        grad_out_w,
        grad_ffn_gain,
        grad_gate_w,
        grad_up_w,
        grad_down_w,
    )


def solution(mesh):
    in_specs = (
        P("dp", None),
        P(),
        P(),
        P(None, "tensor"),
        P(None, "tensor"),
        P(None, "tensor"),
        P(),
        P(),
        P("tensor", None),
        P(),
        P(None, "tensor"),
        P(None, "tensor"),
        P("tensor", None),
        P("dp", None),
    )
    out_specs = (
        P(("dp", "tensor"), None),
        P(("dp", "tensor"), None),
        P("dp"),
        P("dp", "tensor"),
        P("dp", "tensor"),
        P("dp", "tensor"),
        P("dp"),
        P("dp"),
        P("tensor", "dp"),
        P("dp"),
        P("dp", "tensor"),
        P("dp", "tensor"),
        P("tensor", "dp"),
    )
    return jax.shard_map(local, mesh=mesh, in_specs=in_specs, out_specs=out_specs, check_vma=False)
```

```python
import math

import jax
import jax.numpy as jnp
from jax import lax
from jax.experimental import pallas as pl
from jax.experimental.pallas import tpu as pltpu
from jax.sharding import PartitionSpec as P

SEQ_LEN = 2048
EPSILON = 1e-05
ROPE_BASE = 1000000.0
X_SIZE = 4
Y_SIZE = 4
Z_SIZE = 4
TILE = 128
HEAD = 64
APART = 16.0
F32 = jnp.float32
BF16 = jnp.bfloat16

NN = (((1,), (0,)), ((), ()))
NT = (((1,), (1,)), ((), ()))
TN = (((0,), (0,)), ((), ()))


def dot(left, right, dims=NN):
    return lax.dot_general(left, right, dims, preferred_element_type=F32)


def in_sequence(value, steps):
    count = lax.axis_size("dp")
    pairs = [
        (source, source + steps)
        for source in range(count)
        if 0 <= source + steps < count and (source + steps) // X_SIZE == source // X_SIZE
    ]
    return lax.ppermute(value, "dp", pairs)


def over_cores(value):
    count = lax.axis_size("tensor")
    return lax.ppermute(value, "tensor", [(i, i ^ 1) for i in range(count)])


def along_y(value, steps):
    count = lax.axis_size("tensor")
    pairs = [(i, ((i // 2 + steps) % Y_SIZE) * 2 + i % 2) for i in range(count)]
    return lax.ppermute(value, "tensor", pairs)


def gather_relative(value):
    mine = [value] + [along_y(value, k) for k in range(1, Y_SIZE)]
    return [part for kept in mine for part in (kept, over_cores(kept))]


def along_x(value, steps):
    count = lax.axis_size("dp")
    pairs = [(i, i // X_SIZE * X_SIZE + (i % X_SIZE + steps) % X_SIZE) for i in range(count)]
    return lax.ppermute(value, "dp", pairs)


def along_z(value, steps):
    count = lax.axis_size("dp")
    return lax.ppermute(value, "dp", [(i, (i + steps * X_SIZE) % count) for i in range(count)])


def sent_on(values, move):
    return [values[0]] + [move(values[k], k) for k in range(1, len(values))]


def lanes_of(shape):
    return lax.broadcasted_iota(jnp.int32, shape, len(shape) - 1)


def rows_of(shape):
    return lax.broadcasted_iota(jnp.int32, shape, 0)


def halves_swapped(v):
    lane = lanes_of(v.shape) % HEAD
    return jnp.where(lane < HEAD // 2, pltpu.roll(v, 96, 1), pltpu.roll(v, 32, 1))


def other_head(v):
    return pltpu.roll(v, HEAD, 1)


def head_means(v):
    low = lanes_of(v.shape) < HEAD
    first = jnp.sum(jnp.where(low, v, 0.0), axis=-1, keepdims=True)
    second = jnp.sum(jnp.where(low, 0.0, v), axis=-1, keepdims=True)
    return jnp.where(low, first, second) * (1.0 / HEAD)


def unit_of(v):
    inverse = lax.rsqrt(jnp.mean(v * v, axis=-1, keepdims=True) + EPSILON)
    return v * inverse, inverse


def norm_back(grad, unit, inverse, gain):
    grad_unit = grad * gain
    return inverse * (grad_unit - unit * jnp.mean(grad_unit * unit, axis=-1, keepdims=True))


def heads_unit(raw):
    inverse = lax.rsqrt(head_means(raw * raw) + EPSILON)
    return raw * inverse, inverse


def heads_back(grad, unit, inverse, gain):
    grad_unit = grad * gain
    return inverse * (grad_unit - unit * head_means(grad_unit * unit))


def rotated(v, cosine, sine):
    return v * cosine + halves_swapped(v) * sine


def rotated_back(v, cosine, sine):
    return v * cosine - halves_swapped(v) * sine


def call(kernel, operands, outs, scratch=(), far=(), small=(), small_outs=(), limit=4, us=1):
    def spec(i, scalars):
        if i in scalars:
            return pl.BlockSpec(memory_space=pltpu.SMEM)
        return pl.BlockSpec(memory_space=pltpu.VMEM)

    in_specs = [
        pl.BlockSpec(memory_space=pl.ANY) if i in far else spec(i, small)
        for i in range(len(operands))
    ]
    return pl.pallas_call(
        kernel,
        out_shape=[jax.ShapeDtypeStruct(shape, kind) for shape, kind in outs],
        in_specs=in_specs,
        out_specs=[spec(i, small_outs) for i in range(len(outs))],
        scratch_shapes=list(scratch),
        compiler_params=pltpu.CompilerParams(vmem_limit_bytes=limit * 1024 * 1024),
        cost_estimate=pl.CostEstimate(
            flops=us * 10**9, bytes_accessed=us * 10**6, transcendentals=0
        ),
    )(*operands)


def fetch(pairs, sems):
    copies = [pltpu.make_async_copy(a, b, sems.at[i]) for i, (a, b) in enumerate(pairs)]
    for copy in copies:
        copy.start()
    return copies


def wait(copies):
    for copy in copies:
        copy.wait()


def row_of(ref):
    return ref[...].astype(F32).reshape(1, -1)


def place_tables(rows):
    base = (lax.axis_index("dp") % X_SIZE) * rows
    lane = lanes_of((rows // 8, 128))
    rate = jnp.exp((lane % (HEAD // 2)).astype(F32) * (-2.0 / HEAD * math.log(ROPE_BASE)))
    far = (base + 8 * rows_of(lane.shape)).astype(F32) * rate
    near = rows_of((8, 128)).astype(F32) * rate[:8]
    far_c, far_s = jnp.cos(far)[:, None, :], jnp.sin(far)[:, None, :]
    near_c, near_s = jnp.cos(near)[None], jnp.sin(near)[None]
    cosine = (far_c * near_c - far_s * near_s).reshape(rows, 128)
    sine = (far_s * near_c + far_c * near_s).reshape(rows, 128)
    return cosine, jnp.where(lanes_of(sine.shape) % HEAD < HEAD // 2, -sine, sine)


def norm_kv_kernel(tok, gain, wk, wv, kg, normed, packed, raw, cosine, sine):
    rows = tok.shape[0]
    g = row_of(gain)
    for start in range(0, rows, TILE):
        part = pl.ds(start, TILE)
        unit, _ = unit_of(tok[part, :].astype(F32))
        normed[part, :] = (unit * g).astype(BF16)
    weight = jnp.concatenate([wk[...], wv[...]], axis=0)
    kv = dot(normed[...], weight, NT)
    raw[...] = kv
    cosine[...], sine[...] = place_tables(rows)
    unit, _ = heads_unit(kv)
    keys = rotated(unit * two_heads(kg), cosine[...], sine[...])
    packed[...] = jnp.where(lanes_of(kv.shape) < HEAD, keys, kv).astype(BF16)


def two_heads(gain):
    return jnp.concatenate([row_of(gain), row_of(gain)], axis=1)


def query_kernel(
    seg, normed, wq, qg, cosine, sine, cot, wd, meta, low, raw, grad_active, cot_share
):
    q = dot(normed[...], wq[...])
    raw[...] = q
    unit, _ = heads_unit(q)
    low[...] = rotated(unit * two_heads(qg), cosine[...], sine[...]).astype(BF16)
    grad_active[...] = dot(cot[...], wd[...], NT)
    dp, t = lax.axis_index("dp"), lax.axis_index("tensor")
    cot_share[...] = cot[pl.ds(pl.multiple_of(t * 64, 64), 64), :]
    lines = SEQ_LEN // 128
    sequence = seg[pl.ds(pl.multiple_of(dp // X_SIZE * lines, lines), lines), :]
    meta[0] = dp % X_SIZE
    meta[1] = t // 2
    meta[2] = t % 2
    meta[3] = jnp.sum((sequence == jnp.min(sequence)).astype(jnp.int32))
    meta[4] = SEQ_LEN - jnp.sum((sequence == jnp.max(sequence)).astype(jnp.int32))
    meta[5] = dp // X_SIZE
    meta[6] = 0
    meta[7] = 0


def document(place, meta):
    return (place >= meta[3]).astype(jnp.int32) + (place >= meta[4]).astype(jnp.int32)


def key_columns(packed, start, meta):
    shape = packed.shape
    lane = lanes_of(shape)
    mark = jnp.where(lane - HEAD == document(start + rows_of(shape), meta), APART, 0.0)
    return jnp.where(lane < HEAD, packed, mark.astype(BF16))


def value_columns(packed):
    lane = lanes_of(packed.shape)
    return jnp.where(
        lane < HEAD, other_head(packed.astype(F32)), jnp.where(lane < HEAD + 2, 1.0, 0.0)
    ).astype(BF16)


def query_columns(low, start, meta):
    shape = low.shape
    lane = lanes_of(shape)
    wide = low.astype(F32) * (HEAD**-0.5)
    mark = jnp.where(
        (lane - HEAD == document(start + rows_of(shape), meta)) | (lane >= HEAD + 3), 0.0, -APART
    )
    return jnp.concatenate(
        [jnp.where(lane < HEAD, wide, mark), jnp.where(lane < HEAD, other_head(wide), mark)], axis=0
    ).astype(BF16)


def reaches(meta, back, start):
    first_key = (meta[0] - back) * 512
    last_document = document(first_key + 511, meta)
    return (meta[0] >= back) & (last_document >= document(meta[0] * 512 + start, meta))


def attend_kernel(
    meta, low, own, one, two, three, att, output, inverse, key_s, value_s, acc, arrived, sems
):
    rows = low.shape[0]
    copies = fetch([(ref, arrived.at[i]) for i, ref in enumerate((one, two, three))], sems)
    wait(copies)
    pieces = (own, *(arrived.at[i] for i in range(3)))
    for back, piece in enumerate(pieces):

        @pl.when(meta[0] >= back)
        def _(back=back, piece=piece):
            key_s[back] = key_columns(piece[...], (meta[0] - back) * 512, meta)
            value_s[back] = value_columns(piece[...])

    for start in range(0, rows, TILE):
        part = pl.ds(start, TILE)
        queries = query_columns(low[part, :], meta[0] * 512 + start, meta)
        upto = start + TILE
        weights = jnp.exp(dot(queries, key_s[0, pl.ds(start, TILE), :], NT))
        place = rows_of(weights.shape) % TILE
        weights = jnp.where(lanes_of(weights.shape) <= place, weights, 0.0).astype(BF16)
        total = dot(weights, value_s[0, pl.ds(start, TILE), :])
        if start:
            weights = jnp.exp(dot(queries, key_s[0, pl.ds(0, start), :], NT)).astype(BF16)
            total = total + dot(weights, value_s[0, pl.ds(0, start), :])
        acc[...] = total
        for back in range(1, X_SIZE):

            @pl.when(reaches(meta, back, start))
            def _(back=back):
                weights = jnp.exp(dot(queries, key_s[back], NT)).astype(BF16)
                acc[...] += dot(weights, value_s[back])

        total = acc[...]
        inverse_total = 1.0 / total[:, HEAD : HEAD + 1]
        result = total * inverse_total
        lane = lanes_of((TILE, 2 * HEAD))
        both = jnp.where(lane < HEAD, result[:TILE], other_head(result[TILE:]))
        att[part, :] = both.astype(BF16)
        output[part, :] = both
        inverse[part, :] = jnp.where(lane < HEAD, inverse_total[:TILE], inverse_total[TILE:])


def owner(meta, k, c):
    return ((meta[1] + k) % Y_SIZE) * 2 + (meta[2] + c) % 2


def ffn_kernel(meta, *refs):
    att, outw = refs[:8], refs[8:16]
    tok, gain, wg, wu, grad_active = refs[16:21]
    hidden_share, normed, active, grads, keep, give = refs[21:27]
    hidden_s, partial_s, heads_s, weight_s, sems = refs[27:]
    rows, units = grad_active.shape
    pairs = [(w, weight_s.at[pl.ds(i * 128, 128), :]) for i, w in enumerate(outw)]
    for i, a in enumerate(att):
        pairs.append((a, heads_s.at[:, pl.ds(i * 128, 128)]))
    wait(fetch(pairs, sems))
    g = row_of(gain)
    step = 256
    for start in range(0, rows, step):
        part = pl.ds(start, step)
        hidden = tok[part, :].astype(F32) + dot(heads_s[part, :], weight_s[...])
        hidden_s[part, :] = hidden
        unit, _ = unit_of(hidden)
        low = (unit * g).astype(BF16)
        normed[part, :] = low
        gate = dot(low, wg[...], NT)
        upward = dot(low, wu[...], NT)
        sig = jax.nn.sigmoid(gate)
        silu = gate * sig
        active[part, :] = (silu * upward).astype(BF16)
        back = grad_active[part, :]
        grad_gate = (back * upward * sig * (1.0 + gate * (1.0 - sig))).astype(BF16)
        grad_up = (back * silu).astype(BF16)
        grads[part, :] = jnp.concatenate([grad_gate, grad_up], axis=1)
        partial = dot(grad_gate, wg[...]) + dot(grad_up, wu[...])
        partial_s[part, :] = partial.astype(BF16)
    hidden_share[...] = hidden_s[pl.ds(pl.multiple_of(owner(meta, 0, 0) * 64, 64), 64), :]
    split_rows(meta, partial_s, keep, give)


def split_rows(meta, whole, keep, give):
    for k in range(Y_SIZE):
        for c, out in ((0, keep), (1, give)):
            start = pl.multiple_of(owner(meta, k, c) * 64, 64)
            out[k, pl.ds(0, 64), :] = whole[pl.ds(start, 64), :]


def ffn_weights_kernel(meta, normed, grads, cot, active, wd, *refs):
    first, second, (keep, give), (terms_s, chunk) = refs[:4], refs[4:8], refs[8:10], refs[10:]
    wide, units = grads.shape[1], active.shape[1]
    split = first[0].shape[2]
    step = chunk.shape[0]
    for k in range(Z_SIZE):
        z = (meta[5] + k) % Z_SIZE
        part = pl.ds(pl.multiple_of(z * step, step), step)
        chunk[:, pl.ds(0, wide)] = dot(normed[:, part], grads[...], TN).astype(BF16)
        chunk[:, pl.ds(wide, units)] = dot(cot[:, part], active[...], TN).astype(BF16)
        for j in range(X_SIZE):
            start = pl.multiple_of((meta[0] + j) % X_SIZE * 64, 64)
            first[j][z] = chunk[pl.ds(start, 64), pl.ds(0, split)]
            second[k][j] = chunk[pl.ds(j * 64, 64), pl.ds(split, wide + units - split)]
    terms_s[...] = dot(active[...], wd[...]).astype(BF16)
    split_rows(meta, terms_s, keep, give)


def four_summed(own, far, near, copies, index):
    if copies:
        wait(copies)
    total = own[index].astype(F32)
    for i in range(len(far)):
        total = total + near[i, index].astype(F32)
    return total


def early_middle_kernel(meta, *refs):
    (own_a, *far_a), (own_b, *far_b) = refs[:4], refs[4:8]
    first, second, near_a, near_b, sems = refs[8:12], refs[12:16], refs[16], refs[17], refs[18]
    pairs = [(ref, near_a.at[i]) for i, ref in enumerate(far_a)]
    pairs += [(ref, near_b.at[i]) for i, ref in enumerate(far_b)]
    copies = fetch(pairs, sems)
    for k in range(4):
        z, x = (meta[5] + k) % Z_SIZE, (meta[0] + k) % X_SIZE
        total = four_summed(own_a, far_a, near_a, copies if k == 0 else [], z)
        first[k][...] = total.astype(BF16)
        second[k][...] = four_summed(own_b, far_b, near_b, [], x).astype(BF16)


def early_kernel(*refs):
    (own_a, *far_a), (own_b, *far_b) = refs[:4], refs[4:8]
    gate, upward, down, near_a, near_b, sems = refs[8:]
    pairs = [(ref, near_a.at[i]) for i, ref in enumerate(far_a)]
    pairs += [(ref, near_b.at[i]) for i, ref in enumerate(far_b)]
    copies = fetch(pairs, sems)
    total = jnp.concatenate(
        [
            four_summed(own_a, far_a, near_a, copies, ...),
            four_summed(own_b, far_b, near_b, [], ...),
        ],
        axis=1,
    )
    units = gate.shape[1]
    gate[...] = total[:, :units]
    upward[...] = total[:, units : 2 * units]
    down[...] = total[:, 2 * units :]


def late_middle_kernel(meta, own, one, two, three, first, second, third, fourth, near, sems):
    copies = fetch([(ref, near.at[i]) for i, ref in enumerate((one, two, three))], sems)
    for k, out in enumerate((first, second, third, fourth)):
        z = (meta[5] + k) % Z_SIZE
        total = four_summed(own, (one, two, three), near, copies if k == 0 else [], z)
        out[...] = total.astype(BF16)


def late_kernel(own, one, two, three, query, out, key, value, gains, near, sems):
    copies = fetch([(ref, near.at[i]) for i, ref in enumerate((one, two, three))], sems)
    total = four_summed(own, (one, two, three), near, copies, ...)
    wide = query.shape[1]
    query[...] = total[:64, :wide]
    out[...] = total[:64, wide : 2 * wide]
    key[...] = total[:64, 2 * wide : 2 * wide + HEAD]
    value[...] = total[:64, 2 * wide + HEAD :]
    gains[...] = total[64:80, :wide].astype(BF16)


def add_cores_kernel(keep, got, own, one, two, three, got_s, sems):
    wait(fetch([(got, got_s)], sems))
    for k, out in enumerate((own, one, two, three)):
        out[...] = (keep[k].astype(F32) + got_s[k].astype(F32)).astype(out.dtype)


def total_of(own, far, near, sems):
    wait(fetch([(ref, near.at[i]) for i, ref in enumerate(far)], sems))
    return own[...] + near[0].astype(F32) + near[1].astype(F32) + near[2].astype(F32)


def hidden_back_kernel(
    own, one, two, three, hidden, gain, cot, grad_hidden, low, grad_gain, near, sems
):
    grad = total_of(own, (one, two, three), near, sems)
    unit, inverse = unit_of(hidden[...])
    grad_gain[...] = jnp.sum(grad * unit, axis=0, keepdims=True)
    result = cot[...].astype(F32) + norm_back(grad, unit, inverse, row_of(gain))
    grad_hidden[...] = result
    low[...] = result.astype(BF16)


def attend_back_kernel(meta, *refs):
    gathered = refs[:8]
    outw, low, key_s, value_s, output, inverse = refs[8:14]
    whole, grad_q, back_own, back_one, back_two, back_three = refs[14:20]
    grad_k, grad_v, grad_att, acc, sems = refs[20:]
    rows = low.shape[0]
    pairs = []
    for i, part in enumerate(gathered):
        start = pl.multiple_of(owner(meta, -(i // 2) % Y_SIZE, i % 2) * 64, 64)
        pairs.append((part, whole.at[pl.ds(start, 64), :]))
    wait(fetch(pairs, sems))
    grad_att[...] = dot(whole[...], outw[...], NT).astype(BF16)
    grad_k[...] = jnp.zeros_like(grad_k)
    grad_v[...] = jnp.zeros_like(grad_v)
    for start in range(0, rows, TILE):
        part = pl.ds(start, TILE)
        queries = query_columns(low[part, :], meta[0] * 512 + start, meta)
        plain = jnp.concatenate(
            [low[part, :], other_head(low[part, :].astype(F32)).astype(BF16)], axis=0
        )
        scaled = (grad_att[part, :].astype(F32) * inverse[part, :] * (HEAD**-0.5)).astype(BF16)
        wide = scaled.astype(F32)
        products = wide * output[part, :]
        lane = lanes_of((TILE, 2 * HEAD))
        heads = []
        for head in range(2):
            mine = (lane < HEAD) if head == 0 else (lane >= HEAD)
            delta = -jnp.sum(jnp.where(mine, products, 0.0), axis=-1, keepdims=True)
            high = delta.astype(BF16).astype(F32)
            value = wide if head == 0 else other_head(wide)
            heads.append(
                jnp.where(
                    lane < HEAD,
                    value,
                    jnp.where(lane == HEAD, high, jnp.where(lane == HEAD + 1, delta - high, 0.0)),
                )
            )
        grads = jnp.concatenate(heads, axis=0).astype(BF16)

        def block(back, first, count, causal):
            span = pl.ds(first, count)
            keys = key_s[back, span, :]
            weights = jnp.exp(dot(keys, queries, NT))
            if causal:
                place = lanes_of(weights.shape) % TILE
                weights = jnp.where(rows_of(weights.shape) <= place, weights, 0.0)
            grad_v[back, span, :] += dot(weights.astype(BF16), grads)
            scores = (weights * dot(value_s[back, span, :], grads, NT)).astype(BF16)
            grad_k[back, span, :] += dot(scores, plain)
            return dot(scores, keys, TN)

        total = block(0, start, TILE, True)
        if start:
            total = total + block(0, 0, start, False)
        acc[...] = total
        for back in range(1, X_SIZE):

            @pl.when(reaches(meta, back, start))
            def _(back=back):
                acc[...] += block(back, 0, 512, False)

        grad_q[part, :] = jnp.where(lane < HEAD, acc[pl.ds(0, TILE), :], other_head(acc[pl.ds(TILE, TILE), :]))
    for back, out in enumerate((back_own, back_one, back_two, back_three)):
        lane = lanes_of(out.shape)
        values = other_head(grad_v[back]) * (HEAD**0.5)
        out[...] = jnp.where(lane < HEAD, grad_k[back], values).astype(out.dtype)


def query_back_kernel(grad_rot, raw, qg, cosine, sine, normed, whole, att, low, summed, grad_gain):
    grad = rotated_back(grad_rot[...], cosine[...], sine[...])
    unit, inverse = heads_unit(raw[...])
    gain_both = jnp.sum(grad * unit, axis=0, keepdims=True)
    grad_gain[...] = gain_both + other_head(gain_both)
    low[...] = heads_back(grad, unit, inverse, two_heads(qg)).astype(BF16)
    wide = low.shape[1]
    summed[:, :, pl.ds(0, wide)] = dot(normed[...], low[...], TN).astype(BF16).reshape(16, 64, wide)
    summed[:, :, pl.ds(wide, wide)] = (
        dot(whole[...], att[...], TN).astype(BF16).reshape(16, 64, wide)
    )


def key_back_kernel(
    meta, own, one, two, three, raw, kg, cosine, sine, normed, grad_q, wq, wk, wv, tok,
    ffn_gain, q_gain, before, keep_terms, give_terms, first, second, third, fourth, keep, give, summed, partial_s, near, sems,
):
    lane = lanes_of(own.shape)
    rot = total_of(own, (one, two, three), near, sems)
    grad = rotated_back(rot, cosine[...], sine[...])
    unit, inverse = heads_unit(raw[...])
    k_gain = jnp.sum(jnp.where(lane < HEAD, grad * unit, 0.0), axis=0, keepdims=True)
    keys = heads_back(grad, unit, inverse, two_heads(kg))
    low = jnp.where(lane < HEAD, keys, rot).astype(BF16)
    wide = low.shape[1]
    summed[:, pl.ds(0, 64), pl.ds(0, 2 * wide)] = before[...]
    summed[:, pl.ds(0, 64), pl.ds(2 * wide, wide)] = (
        dot(normed[...], low, TN).astype(BF16).reshape(16, 64, wide)
    )
    kv_weight = jnp.concatenate([wk[...], wv[...]], axis=0)
    a_gain = jnp.zeros((1, tok.shape[1]), F32)
    step = 256
    for start in range(0, own.shape[0], step):
        part = pl.ds(start, step)
        partial = dot(grad_q[part, :], wq[...], NT) + dot(low[start : start + step], kv_weight)
        partial_s[part, :] = partial.astype(BF16)
        token_unit, _ = unit_of(tok[part, :].astype(F32))
        a_gain = a_gain + jnp.sum(partial * token_unit, axis=0, keepdims=True)
    split_rows(meta, partial_s, keep, give)
    for k in range(Y_SIZE):
        keep[k, pl.ds(64, 64), :] = keep_terms[k]
        give[k, pl.ds(64, 64), :] = give_terms[k]
    summed[:, pl.ds(64, 16), :] = jnp.zeros((16, 16, 3 * wide), BF16)
    half, rest = jnp.zeros((1, 64), F32), jnp.zeros((12, 128), F32)
    for p in range(16):
        own_rows = [
            jnp.concatenate([gain[:, p * 64 : (p + 1) * 64], half], axis=1)
            for gain in (a_gain, ffn_gain[...])
        ]
        lines = jnp.concatenate([*own_rows, q_gain[...], k_gain, rest], axis=0)
        summed[p, pl.ds(64, 16), pl.ds(0, 128)] = lines.astype(BF16)
    for k, out in enumerate((first, second, third, fourth)):
        for z in range(Z_SIZE):
            out[z] = summed[z * X_SIZE + (meta[0] + k) % X_SIZE]


def final_kernel(
    meta, own, one, two, three, tok, gain, grad_hidden, hidden, grad_tokens, result, near, sems
):
    total = total_of(own, (one, two, three), near, sems)
    mine = tok[pl.ds(pl.multiple_of(owner(meta, 0, 0) * 64, 64), 64), :].astype(F32)
    unit, inverse = unit_of(mine)
    grad_tokens[...] = grad_hidden[...] + norm_back(total[:64], unit, inverse, row_of(gain))
    result[...] = (hidden[...] + total[64:]).astype(BF16)


def gains_kernel(*refs):
    parts, (attn, ffn, query, key) = refs[:8], refs[8:]
    total = 0.0
    for part in parts:
        total = total + part[...].astype(F32)
    attn[...] = total[0:1, :64]
    ffn[...] = total[1:2, :64]
    mine = pltpu.roll(total, 128 - lax.axis_index("dp") * 4, 1)
    query[...] = mine[2:3, :4]
    key[...] = mine[3:4, :4]


def sems(count):
    return pltpu.SemaphoreType.DMA((count,))


def sum_at_owner(keep, give):
    got = over_cores(give)
    shape = keep.shape[1:]
    own, one, two, three = call(
        add_cores_kernel,
        [keep, got],
        [(shape, F32)] + [(shape, BF16)] * 3,
        scratch=[pltpu.VMEM(got.shape, BF16), sems(1)],
        far=(1,),
    )
    return own, along_y(one, 1), along_y(two, 2), along_y(three, 3)


def local(
    tokens, segments, attn_gain, query_weight, key_weight, value_weight, query_gain, key_gain,
    out_weight, ffn_gain, gate_weight, up_weight, down_weight, cotangent,
):
    rows, width = tokens.shape
    units = gate_weight.shape[1]
    key_weight, value_weight = key_weight.T, value_weight.T
    gate_weight, up_weight = gate_weight.T, up_weight.T
    normed, packed, kv_raw, cosine, sine = call(
        norm_kv_kernel,
        [tokens, attn_gain, key_weight, value_weight, key_gain],
        [((rows, width), BF16), ((rows, 128), BF16)] + [((rows, 128), F32)] * 3,
        us=1,
    )
    arrived = [in_sequence(packed, k) for k in range(1, X_SIZE)]
    meta, q_low, q_raw, grad_active, cot_share = call(
        query_kernel,
        [
            segments.reshape(-1, 128), normed, query_weight, query_gain, cosine, sine, cotangent,
            down_weight,
        ],
        [
            ((8,), jnp.int32), ((rows, 128), BF16), ((rows, 128), F32), ((rows, units), F32),
            ((64, width), BF16),
        ],
        small_outs=(0,),
        us=2,
    )
    att, output, inverse, keys, values = call(
        attend_kernel,
        [meta, q_low, packed, *arrived],
        [((rows, 128), BF16), ((rows, 128), F32), ((rows, 128), F32)]
        + [((X_SIZE, rows, 128), BF16)] * 2,
        scratch=[
            pltpu.VMEM((2 * TILE, 128), F32),
            pltpu.VMEM((X_SIZE - 1, rows, 128), BF16),
            sems(3),
        ],
        small=(0,),
        far=(3, 4, 5),
        us=6,
    )
    out_all = gather_relative(out_weight)
    att_all = gather_relative(att)
    hidden_share, normed_two, active, grads, keep, give = call(
        ffn_kernel,
        [meta, *att_all, *out_all, tokens, ffn_gain, gate_weight, up_weight, grad_active],
        [
            ((64, width), F32), ((rows, width), BF16), ((rows, units), BF16),
            ((rows, 2 * units), BF16), ((Y_SIZE, 64, width), BF16), ((Y_SIZE, 64, width), BF16),
        ],
        scratch=[
            pltpu.VMEM((rows, width), F32),
            pltpu.VMEM((rows, width), BF16),
            pltpu.VMEM((rows, width), BF16),
            pltpu.VMEM((width, width), BF16),
            sems(16),
        ],
        small=(0,),
        far=tuple(range(1, 17)),
        limit=12,
        us=7,
    )
    shares = sum_at_owner(keep, give)
    split = 896
    rest = 3 * units - split
    *early_parts, keep_terms, give_terms = call(
        ffn_weights_kernel,
        [meta, normed_two, grads, cotangent, active, down_weight],
        [((Z_SIZE, 64, split), BF16)] * 4
        + [((X_SIZE, 64, rest), BF16)] * 4
        + [((Y_SIZE, 64, width), BF16)] * 2,
        scratch=[pltpu.VMEM((rows, width), BF16), pltpu.VMEM((256, 3 * units), BF16)],
        small=(0,),
        limit=8,
        us=4,
    )
    shares = lax.optimization_barrier((*shares, *early_parts))
    shares, early_parts = shares[:4], shares[4:]
    share = pltpu.VMEM((X_SIZE - 1, 64, width), BF16)
    grad_hidden, grad_hidden_low, grad_ffn_gain = call(
        hidden_back_kernel,
        [*shares, hidden_share, ffn_gain, cot_share],
        [((64, width), F32), ((64, width), BF16), ((1, width), F32)],
        scratch=[share, sems(3)],
        far=(1, 2, 3),
    )
    gathered = gather_relative(grad_hidden_low)
    early_parts = lax.optimization_barrier((gathered[2], *early_parts))[1:]
    early_a = sent_on(early_parts[:4], along_x)
    early_b = sent_on(early_parts[4:], along_z)
    whole, grad_q_rot, back_own, *backs = call(
        attend_back_kernel,
        [meta, *gathered, out_weight, q_low, keys, values, output, inverse],
        [((rows, width), BF16), ((rows, 128), F32), ((rows, 128), F32)]
        + [((rows, 128), BF16)] * 3,
        scratch=[
            pltpu.VMEM((X_SIZE, rows, 128), F32),
            pltpu.VMEM((X_SIZE, rows, 128), F32),
            pltpu.VMEM((rows, 128), BF16),
            pltpu.VMEM((2 * TILE, 128), F32),
            sems(8),
        ],
        small=(0,),
        far=tuple(range(1, 9)),
        limit=12,
        us=11,
    )
    returned = [in_sequence(value, -k - 1) for k, value in enumerate(backs)]
    grad_q_low, late_first, grad_q_gain = call(
        query_back_kernel,
        [grad_q_rot, q_raw, query_gain, cosine, sine, normed, whole, att],
        [((rows, 128), BF16), ((16, 64, 256), BF16), ((1, 128), F32)],
    )
    *late_parts, keep, give = call(
        key_back_kernel,
        [
            meta, back_own, *returned, kv_raw, key_gain, cosine, sine, normed, grad_q_low,
            query_weight, key_weight, value_weight, tokens, grad_ffn_gain, grad_q_gain, late_first,
            keep_terms, give_terms,
        ],
        [((Z_SIZE, 80, 384), BF16)] * 4 + [((Y_SIZE, 128, width), BF16)] * 2,
        scratch=[
            pltpu.VMEM((16, 80, 384), BF16),
            pltpu.VMEM((rows, width), BF16),
            pltpu.VMEM((X_SIZE - 1, rows, 128), BF16),
            sems(3),
        ],
        small=(0,),
        far=(2, 3, 4),
        limit=10,
        us=3,
    )
    late_x = sent_on(late_parts, along_x)
    shares = sum_at_owner(keep, give)
    late_parts = call(
        late_middle_kernel,
        [meta, *late_x],
        [((80, 384), BF16)] * 4,
        scratch=[pltpu.VMEM((X_SIZE - 1, Z_SIZE, 80, 384), BF16), sems(3)],
        small=(0,),
        far=(2, 3, 4),
    )
    late_z = sent_on(late_parts, along_z)
    early_parts = call(
        early_middle_kernel,
        [meta, *early_a, *early_b],
        [((64, split), BF16)] * 4 + [((64, rest), BF16)] * 4,
        scratch=[
            pltpu.VMEM((3, Z_SIZE, 64, split), BF16),
            pltpu.VMEM((3, X_SIZE, 64, rest), BF16),
            sems(6),
        ],
        small=(0,),
        far=(2, 3, 4, 6, 7, 8),
        limit=8,
    )
    early_a = sent_on(early_parts[:4], along_z)
    early_b = sent_on(early_parts[4:], along_x)
    grad_tokens, block_output = call(
        final_kernel,
        [meta, *shares, tokens, attn_gain, grad_hidden, hidden_share],
        [((64, width), F32), ((64, width), BF16)],
        scratch=[pltpu.VMEM((X_SIZE - 1, 128, width), BF16), sems(3)],
        small=(0,),
        far=(2, 3, 4),
    )
    query_grad, out_grad, key_grad, value_grad, gain_parts = call(
        late_kernel,
        late_z,
        [((64, 128), F32), ((64, 128), F32), ((64, 64), F32), ((64, 64), F32), ((16, 128), BF16)],
        scratch=[pltpu.VMEM((3, 80, 384), BF16), sems(3)],
        far=(1, 2, 3),
    )
    gains = call(
        gains_kernel,
        gather_relative(gain_parts),
        [((1, 64), F32), ((1, 64), F32), ((1, 4), F32), ((1, 4), F32)],
    )
    gate_grad, up_grad, down_grad = call(
        early_kernel,
        [*early_a, *early_b],
        [((64, units), F32)] * 3,
        scratch=[pltpu.VMEM((3, 64, split), BF16), pltpu.VMEM((3, 64, rest), BF16), sems(6)],
        far=(1, 2, 3, 5, 6, 7),
    )
    return (
        block_output, grad_tokens, gains[0].reshape(-1), query_grad, key_grad, value_grad,
        gains[2].reshape(-1), gains[3].reshape(-1), out_grad.T, gains[1].reshape(-1), gate_grad,
        up_grad, down_grad.T,
    )


def solution(mesh):
    rows_split, columns_split, copied = P("dp", None), P(None, "tensor"), P()
    in_specs = (
        rows_split, copied, copied, columns_split, columns_split, columns_split, copied, copied,
        P("tensor", None), copied, columns_split, columns_split, P("tensor", None), rows_split,
    )
    both, across = P(("dp", "tensor"), None), P("dp", "tensor")
    out_specs = (
        both, both, P("dp"), across, across, across, P("dp"), P("dp"), P("tensor", "dp"), P("dp"),
        across, across, P("tensor", "dp"),
    )
    return jax.shard_map(local, mesh=mesh, in_specs=in_specs, out_specs=out_specs, check_vma=False)
```

```python
import math

import jax
import jax.numpy as jnp
from jax import lax
from jax.experimental import pallas as pl
from jax.experimental.pallas import tpu as pltpu
from jax.sharding import PartitionSpec as P

SEQ_LEN = 2048
EPSILON = 1e-05
ROPE_BASE = 1000000.0
X_SIZE = 4
Y_SIZE = 4
Z_SIZE = 4
TILE = 128
HEAD = 64
APART = 16.0
F32 = jnp.float32
BF16 = jnp.bfloat16

NN = (((1,), (0,)), ((), ()))
NT = (((1,), (1,)), ((), ()))
TN = (((0,), (0,)), ((), ()))


def dot(left, right, dims=NN):
    return lax.dot_general(left, right, dims, preferred_element_type=F32)


def in_sequence(value, steps):
    count = lax.axis_size("dp")
    pairs = [
        (source, source + steps)
        for source in range(count)
        if 0 <= source + steps < count and (source + steps) // X_SIZE == source // X_SIZE
    ]
    return lax.ppermute(value, "dp", pairs)


def over_cores(value):
    count = lax.axis_size("tensor")
    return lax.ppermute(value, "tensor", [(i, i ^ 1) for i in range(count)])


def along_y(value, steps):
    count = lax.axis_size("tensor")
    pairs = [(i, ((i // 2 + steps) % Y_SIZE) * 2 + i % 2) for i in range(count)]
    return lax.ppermute(value, "tensor", pairs)


def gather_relative(value):
    mine = [value] + [along_y(value, k) for k in range(1, Y_SIZE)]
    return [part for kept in mine for part in (kept, over_cores(kept))]


def along_x(value, steps):
    count = lax.axis_size("dp")
    pairs = [(i, i // X_SIZE * X_SIZE + (i % X_SIZE + steps) % X_SIZE) for i in range(count)]
    return lax.ppermute(value, "dp", pairs)


def along_z(value, steps):
    count = lax.axis_size("dp")
    return lax.ppermute(value, "dp", [(i, (i + steps * X_SIZE) % count) for i in range(count)])


def sent_on(values, move):
    return [values[0]] + [move(values[k], k) for k in range(1, len(values))]


def lanes_of(shape):
    return lax.broadcasted_iota(jnp.int32, shape, len(shape) - 1)


def rows_of(shape):
    return lax.broadcasted_iota(jnp.int32, shape, 0)


def halves_swapped(v):
    lane = lanes_of(v.shape) % HEAD
    return jnp.where(lane < HEAD // 2, pltpu.roll(v, 96, 1), pltpu.roll(v, 32, 1))


def other_head(v):
    return pltpu.roll(v, HEAD, 1)


def head_means(v):
    low = lanes_of(v.shape) < HEAD
    first = jnp.sum(jnp.where(low, v, 0.0), axis=-1, keepdims=True)
    second = jnp.sum(jnp.where(low, 0.0, v), axis=-1, keepdims=True)
    return jnp.where(low, first, second) * (1.0 / HEAD)


def unit_of(v):
    inverse = lax.rsqrt(jnp.mean(v * v, axis=-1, keepdims=True) + EPSILON)
    return v * inverse, inverse


def norm_back(grad, unit, inverse, gain):
    grad_unit = grad * gain
    return inverse * (grad_unit - unit * jnp.mean(grad_unit * unit, axis=-1, keepdims=True))


def heads_unit(raw):
    inverse = lax.rsqrt(head_means(raw * raw) + EPSILON)
    return raw * inverse, inverse


def heads_back(grad, unit, inverse, gain):
    grad_unit = grad * gain
    return inverse * (grad_unit - unit * head_means(grad_unit * unit))


def rotated(v, cosine, sine):
    return v * cosine + halves_swapped(v) * sine


def rotated_back(v, cosine, sine):
    return v * cosine - halves_swapped(v) * sine


def call(kernel, operands, outs, scratch=(), far=(), small=(), small_outs=(), limit=4, us=1):
    def spec(i, scalars):
        if i in scalars:
            return pl.BlockSpec(memory_space=pltpu.SMEM)
        return pl.BlockSpec(memory_space=pltpu.VMEM)

    in_specs = [
        pl.BlockSpec(memory_space=pl.ANY) if i in far else spec(i, small)
        for i in range(len(operands))
    ]
    return pl.pallas_call(
        kernel,
        out_shape=[jax.ShapeDtypeStruct(shape, kind) for shape, kind in outs],
        in_specs=in_specs,
        out_specs=[spec(i, small_outs) for i in range(len(outs))],
        scratch_shapes=list(scratch),
        compiler_params=pltpu.CompilerParams(vmem_limit_bytes=limit * 1024 * 1024),
        cost_estimate=pl.CostEstimate(
            flops=us * 10**9, bytes_accessed=us * 10**6, transcendentals=0
        ),
    )(*operands)


def fetch(pairs, sems):
    copies = [pltpu.make_async_copy(a, b, sems.at[i]) for i, (a, b) in enumerate(pairs)]
    for copy in copies:
        copy.start()
    return copies


def wait(copies):
    for copy in copies:
        copy.wait()


def row_of(ref):
    return ref[...].astype(F32).reshape(1, -1)


def place_tables(rows):
    base = (lax.axis_index("dp") % X_SIZE) * rows
    lane = lanes_of((rows // 8, 128))
    rate = jnp.exp((lane % (HEAD // 2)).astype(F32) * (-2.0 / HEAD * math.log(ROPE_BASE)))
    far = (base + 8 * rows_of(lane.shape)).astype(F32) * rate
    near = rows_of((8, 128)).astype(F32) * rate[:8]
    far_c, far_s = jnp.cos(far)[:, None, :], jnp.sin(far)[:, None, :]
    near_c, near_s = jnp.cos(near)[None], jnp.sin(near)[None]
    cosine = (far_c * near_c - far_s * near_s).reshape(rows, 128)
    sine = (far_s * near_c + far_c * near_s).reshape(rows, 128)
    return cosine, jnp.where(lanes_of(sine.shape) % HEAD < HEAD // 2, -sine, sine)


def norm_kv_kernel(tok, gain, wk, wv, kg, normed, packed, raw, cosine, sine):
    rows = tok.shape[0]
    g = row_of(gain)
    for start in range(0, rows, TILE):
        part = pl.ds(start, TILE)
        unit, _ = unit_of(tok[part, :].astype(F32))
        normed[part, :] = (unit * g).astype(BF16)
    weight = jnp.concatenate([wk[...], wv[...]], axis=0)
    kv = dot(normed[...], weight, NT)
    raw[...] = kv
    cosine[...], sine[...] = place_tables(rows)
    unit, _ = heads_unit(kv)
    keys = rotated(unit * two_heads(kg), cosine[...], sine[...])
    packed[...] = jnp.where(lanes_of(kv.shape) < HEAD, keys, kv).astype(BF16)


def two_heads(gain):
    return jnp.concatenate([row_of(gain), row_of(gain)], axis=1)


def query_kernel(
    seg, normed, wq, qg, cosine, sine, cot, wd, meta, low, raw, grad_active, cot_share
):
    q = dot(normed[...], wq[...])
    raw[...] = q
    unit, _ = heads_unit(q)
    low[...] = rotated(unit * two_heads(qg), cosine[...], sine[...]).astype(BF16)
    grad_active[...] = dot(cot[...], wd[...], NT)
    dp, t = lax.axis_index("dp"), lax.axis_index("tensor")
    cot_share[...] = cot[pl.ds(pl.multiple_of(t * 64, 64), 64), :]
    lines = SEQ_LEN // 128
    sequence = seg[pl.ds(pl.multiple_of(dp // X_SIZE * lines, lines), lines), :]
    meta[0] = dp % X_SIZE
    meta[1] = t // 2
    meta[2] = t % 2
    meta[3] = jnp.sum((sequence == jnp.min(sequence)).astype(jnp.int32))
    meta[4] = SEQ_LEN - jnp.sum((sequence == jnp.max(sequence)).astype(jnp.int32))
    meta[5] = dp // X_SIZE
    meta[6] = 0
    meta[7] = 0


def document(place, meta):
    return (place >= meta[3]).astype(jnp.int32) + (place >= meta[4]).astype(jnp.int32)


def key_columns(packed, start, meta):
    shape = packed.shape
    lane = lanes_of(shape)
    mark = jnp.where(lane - HEAD == document(start + rows_of(shape), meta), APART, 0.0)
    return jnp.where(lane < HEAD, packed, mark.astype(BF16))


def value_columns(packed):
    lane = lanes_of(packed.shape)
    return jnp.where(
        lane < HEAD, other_head(packed.astype(F32)), jnp.where(lane < HEAD + 2, 1.0, 0.0)
    ).astype(BF16)


def query_columns(low, start, meta):
    shape = low.shape
    lane = lanes_of(shape)
    wide = low.astype(F32) * (HEAD**-0.5)
    mark = jnp.where(
        (lane - HEAD == document(start + rows_of(shape), meta)) | (lane >= HEAD + 3), 0.0, -APART
    )
    return jnp.concatenate(
        [jnp.where(lane < HEAD, wide, mark), jnp.where(lane < HEAD, other_head(wide), mark)], axis=0
    ).astype(BF16)


def reaches(meta, back, start):
    first_key = (meta[0] - back) * 512
    last_document = document(first_key + 511, meta)
    return (meta[0] >= back) & (last_document >= document(meta[0] * 512 + start, meta))


def attend_kernel(
    meta, low, own, one, two, three, att, output, inverse, key_s, value_s, arrived, sems
):
    rows = low.shape[0]
    copies = fetch([(ref, arrived.at[i]) for i, ref in enumerate((one, two, three))], sems)
    wait(copies)
    pieces = (own, *(arrived.at[i] for i in range(3)))
    for back, piece in enumerate(pieces):

        @pl.when(meta[0] >= back)
        def _(back=back, piece=piece):
            span = pl.ds(back * rows, rows)
            key_s[span, :] = key_columns(piece[...], (meta[0] - back) * rows, meta)
            value_s[span, :] = value_columns(piece[...])

    for start in range(0, rows, TILE):
        reached = pieces_reached(meta, start)
        for count in range(X_SIZE):

            @pl.when(reached == count)
            def _(start=start, count=count):
                part = pl.ds(start, TILE)
                queries = query_columns(low[part, :], meta[0] * rows + start, meta)

                def weighted(first, size, causal):
                    span = pl.ds(first, size)
                    weights = jnp.exp(dot(queries, key_s[span, :], NT))
                    if causal:
                        place = rows_of(weights.shape) % TILE
                        weights = jnp.where(lanes_of(weights.shape) <= place, weights, 0.0)
                    return dot(weights.astype(BF16), value_s[span, :])

                total = weighted(start, TILE, True)
                if start:
                    total = total + weighted(0, start, False)
                if count:
                    total = total + weighted(rows, count * rows, False)
                inverse_total = 1.0 / total[:, HEAD : HEAD + 1]
                result = total * inverse_total
                lane = lanes_of((TILE, 2 * HEAD))
                both = jnp.where(lane < HEAD, result[:TILE], other_head(result[TILE:]))
                att[part, :] = both.astype(BF16)
                output[part, :] = both
                inverse[part, :] = jnp.where(
                    lane < HEAD, inverse_total[:TILE], inverse_total[TILE:]
                )


def pieces_reached(meta, start):
    return sum(reaches(meta, back, start).astype(jnp.int32) for back in range(1, X_SIZE))


def owner(meta, k, c):
    return ((meta[1] + k) % Y_SIZE) * 2 + (meta[2] + c) % 2


def ffn_kernel(meta, *refs):
    att, outw = refs[:8], refs[8:16]
    tok, gain, wg, wu, grad_active = refs[16:21]
    hidden_share, normed, active, grads, keep, give = refs[21:27]
    hidden_s, partial_s, heads_s, weight_s, sems = refs[27:]
    rows, units = grad_active.shape
    pairs = [(w, weight_s.at[pl.ds(i * 128, 128), :]) for i, w in enumerate(outw)]
    for i, a in enumerate(att):
        pairs.append((a, heads_s.at[:, pl.ds(i * 128, 128)]))
    wait(fetch(pairs, sems))
    g = row_of(gain)
    step = 256
    for start in range(0, rows, step):
        part = pl.ds(start, step)
        hidden = tok[part, :].astype(F32) + dot(heads_s[part, :], weight_s[...])
        hidden_s[part, :] = hidden
        unit, _ = unit_of(hidden)
        low = (unit * g).astype(BF16)
        normed[part, :] = low
        gate = dot(low, wg[...], NT)
        upward = dot(low, wu[...], NT)
        sig = jax.nn.sigmoid(gate)
        silu = gate * sig
        active[part, :] = (silu * upward).astype(BF16)
        back = grad_active[part, :]
        grad_gate = (back * upward * sig * (1.0 + gate * (1.0 - sig))).astype(BF16)
        grad_up = (back * silu).astype(BF16)
        grads[part, :] = jnp.concatenate([grad_gate, grad_up], axis=1)
        partial = dot(grad_gate, wg[...]) + dot(grad_up, wu[...])
        partial_s[part, :] = partial.astype(BF16)
    hidden_share[...] = hidden_s[pl.ds(pl.multiple_of(owner(meta, 0, 0) * 64, 64), 64), :]
    split_rows(meta, partial_s, keep, give)


def split_rows(meta, whole, keep, give):
    for k in range(Y_SIZE):
        for c, out in ((0, keep), (1, give)):
            start = pl.multiple_of(owner(meta, k, c) * 64, 64)
            out[k, pl.ds(0, 64), :] = whole[pl.ds(start, 64), :]


def ffn_weights_kernel(meta, normed, grads, cot, active, wd, *refs):
    outs, (far_up, far_down, keep, give), (chunk, terms_s) = refs[:3], refs[3:7], refs[7:]
    wide, units = grads.shape[1], active.shape[1]
    step = chunk.shape[0]
    for k, out in enumerate((outs[0], outs[1], chunk, outs[2])):
        z = (meta[5] + k) % Z_SIZE
        part = pl.ds(pl.multiple_of(z * step, step), step)
        out[:, pl.ds(0, wide)] = dot(normed[:, part], grads[...], TN).astype(BF16)
        out[:, pl.ds(wide, units)] = dot(cot[:, part], active[...], TN).astype(BF16)
        rest = out.shape[1] - wide - units
        out[:, pl.ds(wide + units, rest)] = jnp.zeros((step, rest), BF16)
    half = far_up.shape[1]
    far_up[...] = chunk[:, pl.ds(0, half)]
    far_down[...] = chunk[:, pl.ds(half, half)]
    terms_s[...] = dot(active[...], wd[...]).astype(BF16)
    split_rows(meta, terms_s, keep, give)


def relay_kernel(near_up, near_down, far_up, far_down, up, down, after, got, sems):
    after[...] = jnp.zeros_like(after)
    copies = fetch([(far_up, got.at[0]), (far_down, got.at[1])], sems)
    half = far_up.shape[1]
    lower, upper = pl.ds(0, half), pl.ds(half, half)
    up[:, upper] = near_up[:, upper]
    down[:, lower] = near_down[:, lower]
    wait(copies)
    for start in range(0, up.shape[0], 64):
        part = pl.ds(start, 64)
        up[part, lower] = (near_up[part, lower].astype(F32) + got[0, part, :].astype(F32)).astype(BF16)
        down[part, upper] = (
            near_down[part, upper].astype(F32) + got[1, part, :].astype(F32)
        ).astype(BF16)


def early_sum_kernel(own, one, two, total, after, near, sems):
    after[...] = jnp.zeros_like(after)
    wait(fetch([(one, near.at[0]), (two, near.at[1])], sems))
    for start in range(0, own.shape[0], 64):
        part = pl.ds(start, 64)
        total[part, :] = (
            own[part, :].astype(F32) + near[0, part, :].astype(F32) + near[1, part, :].astype(F32)
        ).astype(BF16)


def middle_kernel(meta, early, own, *refs):
    far, outs, (near, sems) = refs[:3], refs[3:7], refs[7:]
    wait(fetch([(ref, near.at[i]) for i, ref in enumerate(far)], sems))
    wide = early.shape[1]
    for k, out in enumerate(outs):
        x = (meta[0] + k) % X_SIZE
        part = pl.ds(pl.multiple_of(x * 64, 64), 64)
        out[:, pl.ds(0, wide)] = early[part, :]
        total = own[x].astype(F32)
        for i in range(3):
            total = total + near[i, x].astype(F32)
        out[:, pl.ds(wide, own.shape[2])] = total.astype(BF16)


def weights_kernel(
    own, one, two, three, before, gate, upward, down, query, out, key, value, gains, near, sems
):
    wait(fetch([(ref, near.at[i]) for i, ref in enumerate((one, two, three))], sems))
    total = own[...].astype(F32)
    for i in range(3):
        total = total + near[i].astype(F32)
    units = gate.shape[1]
    gate[...] = total[:, :units]
    upward[...] = total[:, units : 2 * units]
    down[...] = total[:, 2 * units : 3 * units]
    start = total.shape[1] - 512
    query[...] = total[:, start : start + 128]
    out[...] = total[:, start + 128 : start + 256]
    key[...] = total[:, start + 256 : start + 320]
    value[...] = total[:, start + 320 : start + 384]
    gains[...] = total[:16, start + 384 :].astype(BF16)


def add_cores_kernel(keep, got, own, one, two, three, got_s, sems):
    wait(fetch([(got, got_s)], sems))
    for k, out in enumerate((own, one, two, three)):
        out[...] = (keep[k].astype(F32) + got_s[k].astype(F32)).astype(out.dtype)


def total_of(own, far, near, sems):
    wait(fetch([(ref, near.at[i]) for i, ref in enumerate(far)], sems))
    return own[...] + near[0].astype(F32) + near[1].astype(F32) + near[2].astype(F32)


def hidden_back_kernel(
    own, one, two, three, hidden, gain, cot, grad_hidden, low, grad_gain, near, sems
):
    grad = total_of(own, (one, two, three), near, sems)
    unit, inverse = unit_of(hidden[...])
    grad_gain[...] = jnp.sum(grad * unit, axis=0, keepdims=True)
    result = cot[...].astype(F32) + norm_back(grad, unit, inverse, row_of(gain))
    grad_hidden[...] = result
    low[...] = result.astype(BF16)


def attend_back_rows(
    meta, start, low, key_s, value_s, output, inverse, grad_att, grad_k, grad_v, grad_q, acc
):
    rows = low.shape[0]
    part = pl.ds(start, TILE)
    queries = query_columns(low[part, :], meta[0] * rows + start, meta)
    plain = jnp.concatenate(
        [low[part, :], other_head(low[part, :].astype(F32)).astype(BF16)], axis=0
    )
    scaled = (grad_att[part, :].astype(F32) * inverse[part, :] * (HEAD**-0.5)).astype(BF16)
    wide = scaled.astype(F32)
    products = wide * output[part, :]
    lane = lanes_of((TILE, 2 * HEAD))
    heads = []
    for head in range(2):
        mine = (lane < HEAD) if head == 0 else (lane >= HEAD)
        delta = -jnp.sum(jnp.where(mine, products, 0.0), axis=-1, keepdims=True)
        high = delta.astype(BF16).astype(F32)
        value = wide if head == 0 else other_head(wide)
        rest = jnp.where(lane == HEAD, high, jnp.where(lane == HEAD + 1, delta - high, 0.0))
        heads.append(jnp.where(lane < HEAD, value, rest))
    grads = jnp.concatenate(heads, axis=0).astype(BF16)

    def block(first, size, causal):
        span = pl.ds(first, size)
        keys = key_s[span, :]
        weights = jnp.exp(dot(keys, queries, NT))
        if causal:
            place = lanes_of(weights.shape) % TILE
            weights = jnp.where(rows_of(weights.shape) <= place, weights, 0.0)
        grad_v[span, :] += dot(weights.astype(BF16), grads)
        scores = (weights * dot(value_s[span, :], grads, NT)).astype(BF16)
        grad_k[span, :] += dot(scores, plain)
        return dot(scores, keys, TN)

    total = block(start, TILE, True)
    if start:
        total = total + block(0, start, False)
    acc[...] = total
    for back in range(1, X_SIZE):

        @pl.when(reaches(meta, back, start))
        def _(back=back):
            acc[...] += block(back * rows, rows, False)

    grad_q[part, :] = jnp.where(
        lane < HEAD, acc[pl.ds(0, TILE), :], other_head(acc[pl.ds(TILE, TILE), :])
    )


def attend_back_kernel(meta, *refs):
    gathered = refs[:8]
    outw, low, key_s, value_s, output, inverse = refs[8:14]
    whole, grad_q, back_own, back_one, back_two, back_three = refs[15:21]
    grad_k, grad_v, grad_att, acc, sems = refs[21:]
    rows = low.shape[0]
    pairs = []
    for i, part in enumerate(gathered):
        start = pl.multiple_of(owner(meta, -(i // 2) % Y_SIZE, i % 2) * 64, 64)
        pairs.append((part, whole.at[pl.ds(start, 64), :]))
    wait(fetch(pairs, sems))
    grad_att[...] = dot(whole[...], outw[...], NT).astype(BF16)
    grad_k[...] = jnp.zeros_like(grad_k)
    grad_v[...] = jnp.zeros_like(grad_v)
    for start in range(0, rows, TILE):
        attend_back_rows(
            meta, start, low, key_s, value_s, output, inverse, grad_att, grad_k, grad_v, grad_q, acc
        )

    for back, out in enumerate((back_own, back_one, back_two, back_three)):
        lane = lanes_of(out.shape)
        span = pl.ds(back * rows, rows)
        values = other_head(grad_v[span, :]) * (HEAD**0.5)
        out[...] = jnp.where(lane < HEAD, grad_k[span, :], values).astype(out.dtype)


def query_back_kernel(
    grad_rot, raw, qg, cosine, sine, normed, whole, att, low, summed, grad_gain
):
    grad = rotated_back(grad_rot[...], cosine[...], sine[...])
    unit, inverse = heads_unit(raw[...])
    gain_both = jnp.sum(grad * unit, axis=0, keepdims=True)
    grad_gain[...] = gain_both + other_head(gain_both)
    low[...] = heads_back(grad, unit, inverse, two_heads(qg)).astype(BF16)
    wide = low.shape[1]
    summed[:, :, pl.ds(0, wide)] = dot(normed[...], low[...], TN).astype(BF16).reshape(16, 64, wide)
    summed[:, :, pl.ds(wide, wide)] = (
        dot(whole[...], att[...], TN).astype(BF16).reshape(16, 64, wide)
    )


def key_back_kernel(
    meta, own, one, two, three, raw, kg, cosine, sine, normed, grad_q, wq, wk, wv, tok,
    ffn_gain, q_gain, before, keep_terms, give_terms, before_this, first, second, third, fourth, keep, give, summed, partial_s, near, sems,
):
    lane = lanes_of(own.shape)
    rot = total_of(own, (one, two, three), near, sems)
    grad = rotated_back(rot, cosine[...], sine[...])
    unit, inverse = heads_unit(raw[...])
    k_gain = jnp.sum(jnp.where(lane < HEAD, grad * unit, 0.0), axis=0, keepdims=True)
    keys = heads_back(grad, unit, inverse, two_heads(kg))
    low = jnp.where(lane < HEAD, keys, rot).astype(BF16)
    wide = low.shape[1]
    summed[:, :, pl.ds(0, 2 * wide)] = before[...]
    summed[:, :, pl.ds(2 * wide, wide)] = (
        dot(normed[...], low, TN).astype(BF16).reshape(16, 64, wide)
    )
    kv_weight = jnp.concatenate([wk[...], wv[...]], axis=0)
    a_gain = jnp.zeros((1, tok.shape[1]), F32)
    step = 256
    for start in range(0, own.shape[0], step):
        part = pl.ds(start, step)
        partial = dot(grad_q[part, :], wq[...], NT) + dot(low[start : start + step], kv_weight)
        partial_s[part, :] = partial.astype(BF16)
        token_unit, _ = unit_of(tok[part, :].astype(F32))
        a_gain = a_gain + jnp.sum(partial * token_unit, axis=0, keepdims=True)
    split_rows(meta, partial_s, keep, give)
    for k in range(Y_SIZE):
        keep[k, pl.ds(64, 64), :] = keep_terms[k]
        give[k, pl.ds(64, 64), :] = give_terms[k]
    summed[:, :, pl.ds(3 * wide, wide)] = jnp.zeros((16, 64, wide), BF16)
    half, rest = jnp.zeros((1, 64), F32), jnp.zeros((12, 128), F32)
    for p in range(16):
        own_rows = [
            jnp.concatenate([gain[:, p * 64 : (p + 1) * 64], half], axis=1)
            for gain in (a_gain, ffn_gain[...])
        ]
        lines = jnp.concatenate([*own_rows, q_gain[...], k_gain, rest], axis=0)
        summed[p, pl.ds(0, 16), pl.ds(3 * wide, wide)] = lines.astype(BF16)
    for k, out in enumerate((first, second, third, fourth)):
        out[...] = summed[pl.ds((meta[5] + k) % Z_SIZE * X_SIZE, X_SIZE)]


def final_kernel(
    meta, own, one, two, three, tok, gain, grad_hidden, hidden, grad_tokens, result, after, near, sems
):
    after[...] = jnp.zeros_like(after)
    total = total_of(own, (one, two, three), near, sems)
    mine = tok[pl.ds(pl.multiple_of(owner(meta, 0, 0) * 64, 64), 64), :].astype(F32)
    unit, inverse = unit_of(mine)
    grad_tokens[...] = grad_hidden[...] + norm_back(total[:64], unit, inverse, row_of(gain))
    result[...] = (hidden[...] + total[64:]).astype(BF16)


def gains_kernel(*refs):
    parts, (attn, ffn, query, key) = refs[:8], refs[8:]
    total = 0.0
    for part in parts:
        total = total + part[...].astype(F32)
    attn[...] = total[0:1, :64]
    ffn[...] = total[1:2, :64]
    mine = pltpu.roll(total, 128 - lax.axis_index("dp") * 4, 1)
    query[...] = mine[2:3, :4]
    key[...] = mine[3:4, :4]


def sems(count):
    return pltpu.SemaphoreType.DMA((count,))


def sum_at_owner(keep, give):
    got = over_cores(give)
    shape = keep.shape[1:]
    own, one, two, three = call(
        add_cores_kernel,
        [keep, got],
        [(shape, F32)] + [(shape, BF16)] * 3,
        scratch=[pltpu.VMEM(got.shape, BF16), sems(1)],
        far=(1,),
    )
    return own, along_y(one, 1), along_y(two, 2), along_y(three, 3)


def local(
    tokens, segments, attn_gain, query_weight, key_weight, value_weight, query_gain, key_gain,
    out_weight, ffn_gain, gate_weight, up_weight, down_weight, cotangent,
):
    rows, width = tokens.shape
    units = gate_weight.shape[1]
    early_wide = -(-3 * units // 128) * 128
    key_weight, value_weight = key_weight.T, value_weight.T
    gate_weight, up_weight = gate_weight.T, up_weight.T
    normed, packed, kv_raw, cosine, sine = call(
        norm_kv_kernel,
        [tokens, attn_gain, key_weight, value_weight, key_gain],
        [((rows, width), BF16), ((rows, 128), BF16)] + [((rows, 128), F32)] * 3,
    )
    arrived = [in_sequence(packed, k) for k in range(1, X_SIZE)]
    out_here = lax.optimization_barrier((packed, out_weight))[1]
    meta, q_low, q_raw, grad_active, cot_share = call(
        query_kernel,
        [
            segments.reshape(-1, 128), normed, query_weight, query_gain, cosine, sine, cotangent,
            down_weight,
        ],
        [
            ((8,), jnp.int32), ((rows, 128), BF16), ((rows, 128), F32), ((rows, units), F32),
            ((64, width), BF16),
        ],
        small_outs=(0,),
        us=2,
    )
    att, output, inverse, keys, values = call(
        attend_kernel,
        [meta, q_low, packed, *arrived],
        [((rows, 128), BF16), ((rows, 128), F32), ((rows, 128), F32)]
        + [((X_SIZE * rows, 128), BF16)] * 2,
        scratch=[
            pltpu.VMEM((X_SIZE - 1, rows, 128), BF16),
            sems(3),
        ],
        small=(0,),
        far=(3, 4, 5),
        us=6,
    )
    out_all = gather_relative(out_here)
    att_all = gather_relative(att)
    hidden_share, normed_two, active, grads, keep, give = call(
        ffn_kernel,
        [meta, *att_all, *out_all, tokens, ffn_gain, gate_weight, up_weight, grad_active],
        [
            ((64, width), F32), ((rows, width), BF16), ((rows, units), BF16),
            ((rows, 2 * units), BF16), ((Y_SIZE, 64, width), BF16), ((Y_SIZE, 64, width), BF16),
        ],
        scratch=[
            pltpu.VMEM((rows, width), F32),
            pltpu.VMEM((rows, width), BF16),
            pltpu.VMEM((rows, width), BF16),
            pltpu.VMEM((width, width), BF16),
            sems(16),
        ],
        small=(0,),
        far=tuple(range(1, 17)),
        limit=12,
        us=7,
    )
    shares = sum_at_owner(keep, give)
    *early_parts, keep_terms, give_terms = call(
        ffn_weights_kernel,
        [meta, normed_two, grads, cotangent, active, down_weight],
        [((256, early_wide), BF16)] * 3
        + [((256, early_wide // 2), BF16)] * 2
        + [((Y_SIZE, 64, width), BF16)] * 2,
        scratch=[pltpu.VMEM((256, early_wide), BF16), pltpu.VMEM((rows, width), BF16)],
        small=(0,),
        limit=8,
        us=4,
    )
    shares = lax.optimization_barrier((*shares, *early_parts))
    shares, early_parts = shares[:4], shares[4:]
    share = pltpu.VMEM((X_SIZE - 1, 64, width), BF16)
    grad_hidden, grad_hidden_low, grad_ffn_gain = call(
        hidden_back_kernel,
        [*shares, hidden_share, ffn_gain, cot_share],
        [((64, width), F32), ((64, width), BF16), ((1, width), F32)],
        scratch=[share, sems(3)],
        far=(1, 2, 3),
    )
    gathered = gather_relative(grad_hidden_low)
    own_chunk, near_up, near_down, far_up, far_down = early_parts
    up, down, relay_done = call(
        relay_kernel,
        [near_up, near_down, along_z(far_up, 1), along_z(far_down, -1)],
        [((256, early_wide), BF16)] * 2 + [((8, 128), F32)],
        scratch=[pltpu.VMEM((2, 256, early_wide // 2), BF16), sems(2)],
        far=(2, 3),
    )
    early = [own_chunk, along_z(up, 1), along_z(down, -1)]
    whole, grad_q_rot, back_own, *backs = call(
        attend_back_kernel,
        [meta, *gathered, out_weight, q_low, keys, values, output, inverse, relay_done],
        [((rows, width), BF16), ((rows, 128), F32), ((rows, 128), F32)]
        + [((rows, 128), BF16)] * 3,
        scratch=[
            pltpu.VMEM((X_SIZE * rows, 128), F32),
            pltpu.VMEM((X_SIZE * rows, 128), F32),
            pltpu.VMEM((rows, 128), BF16),
            pltpu.VMEM((2 * TILE, 128), F32),
            sems(8),
        ],
        small=(0,),
        far=tuple(range(1, 9)),
        limit=12,
        us=8,
    )
    returned = [in_sequence(value, -k - 1) for k, value in enumerate(backs)]
    grad_q_low, late_first, grad_q_gain = call(
        query_back_kernel,
        [grad_q_rot, q_raw, query_gain, cosine, sine, normed, whole, att],
        [((rows, 128), BF16), ((16, 64, 256), BF16), ((1, 128), F32)],
    )
    early_sum, early_done = call(
        early_sum_kernel,
        early,
        [((256, early_wide), BF16), ((8, 128), F32)],
        scratch=[pltpu.VMEM((2, 256, early_wide), BF16), sems(2)],
        far=(1, 2),
    )
    *late_parts, keep, give = call(
        key_back_kernel,
        [
            meta, back_own, *returned, kv_raw, key_gain, cosine, sine, normed, grad_q_low,
            query_weight, key_weight, value_weight, tokens, grad_ffn_gain, grad_q_gain, late_first,
            keep_terms, give_terms, early_done,
        ],
        [((X_SIZE, 64, 512), BF16)] * 4 + [((Y_SIZE, 128, width), BF16)] * 2,
        scratch=[
            pltpu.VMEM((16, 64, 512), BF16),
            pltpu.VMEM((rows, width), BF16),
            pltpu.VMEM((X_SIZE - 1, rows, 128), BF16),
            sems(3),
        ],
        small=(0,),
        far=(2, 3, 4),
        limit=10,
        us=3,
    )
    late = sent_on(late_parts, along_z)
    grad_tokens, block_output, rows_done = call(
        final_kernel,
        [meta, *sum_at_owner(keep, give), tokens, attn_gain, grad_hidden, hidden_share],
        [((64, width), F32), ((64, width), BF16), ((8, 128), F32)],
        scratch=[pltpu.VMEM((X_SIZE - 1, 128, width), BF16), sems(3)],
        small=(0,),
        far=(2, 3, 4),
    )
    all_wide = early_wide + 512
    parts = sent_on(
        call(
            middle_kernel,
            [meta, early_sum, *late],
            [((64, all_wide), BF16)] * 4,
            scratch=[
                pltpu.VMEM((3, X_SIZE, 64, 512), BF16),
                sems(3),
            ],
            small=(0,),
            far=(3, 4, 5),
        ),
        along_x,
    )
    gate_grad, up_grad, down_grad, query_grad, out_grad, key_grad, value_grad, gain_parts = call(
        weights_kernel,
        [*parts, rows_done],
        [((64, units), F32)] * 3
        + [((64, 128), F32), ((64, 128), F32), ((64, 64), F32), ((64, 64), F32), ((16, 128), BF16)],
        scratch=[pltpu.VMEM((3, 64, all_wide), BF16), sems(3)],
        far=(1, 2, 3),
    )
    gains = call(
        gains_kernel,
        gather_relative(gain_parts),
        [((1, 64), F32), ((1, 64), F32), ((1, 4), F32), ((1, 4), F32)],
    )
    return (
        block_output, grad_tokens, gains[0].reshape(-1), query_grad, key_grad, value_grad,
        gains[2].reshape(-1), gains[3].reshape(-1), out_grad.T, gains[1].reshape(-1), gate_grad,
        up_grad, down_grad.T,
    )


def solution(mesh):
    rows_split, columns_split, copied = P("dp", None), P(None, "tensor"), P()
    in_specs = (
        rows_split, copied, copied, columns_split, columns_split, columns_split, copied, copied,
        P("tensor", None), copied, columns_split, columns_split, P("tensor", None), rows_split,
    )
    both, across = P(("dp", "tensor"), None), P("dp", "tensor")
    out_specs = (
        both, both, P("dp"), across, across, across, P("dp"), P("dp"), P("tensor", "dp"), P("dp"),
        across, across, P("tensor", "dp"),
    )
    return jax.shard_map(local, mesh=mesh, in_specs=in_specs, out_specs=out_specs, check_vma=False)
```

```python
import math

import jax
import jax.numpy as jnp
from jax import lax
from jax.experimental import pallas as pl
from jax.experimental.pallas import tpu as pltpu
from jax.sharding import PartitionSpec as P

SEQ_LEN = 2048
EPSILON = 1e-05
ROPE_BASE = 1000000.0
X_SIZE = 4
Y_SIZE = 4
Z_SIZE = 4
TILE = 128
HEAD = 64
APART = 16.0
F32 = jnp.float32
BF16 = jnp.bfloat16

NN = (((1,), (0,)), ((), ()))
NT = (((1,), (1,)), ((), ()))
TN = (((0,), (0,)), ((), ()))


def dot(left, right, dims=NN):
    return lax.dot_general(left, right, dims, preferred_element_type=F32)


def in_sequence(value, steps):
    count = lax.axis_size("dp")
    pairs = [
        (source, source + steps)
        for source in range(count)
        if 0 <= source + steps < count and (source + steps) // X_SIZE == source // X_SIZE
    ]
    return lax.ppermute(value, "dp", pairs)


def over_cores(value):
    count = lax.axis_size("tensor")
    return lax.ppermute(value, "tensor", [(i, i ^ 1) for i in range(count)])


def along_y(value, steps):
    count = lax.axis_size("tensor")
    pairs = [(i, ((i // 2 + steps) % Y_SIZE) * 2 + i % 2) for i in range(count)]
    return lax.ppermute(value, "tensor", pairs)


def gather_relative(value):
    mine = [value] + [along_y(value, k) for k in range(1, Y_SIZE)]
    return [part for kept in mine for part in (kept, over_cores(kept))]


def along_x(value, steps):
    count = lax.axis_size("dp")
    pairs = [(i, i // X_SIZE * X_SIZE + (i % X_SIZE + steps) % X_SIZE) for i in range(count)]
    return lax.ppermute(value, "dp", pairs)


def along_z(value, steps):
    count = lax.axis_size("dp")
    return lax.ppermute(value, "dp", [(i, (i + steps * X_SIZE) % count) for i in range(count)])


def sent_on(values, move):
    return [values[0]] + [move(values[k], k) for k in range(1, len(values))]


def lanes_of(shape):
    return lax.broadcasted_iota(jnp.int32, shape, len(shape) - 1)


def rows_of(shape):
    return lax.broadcasted_iota(jnp.int32, shape, 0)


def halves_swapped(v):
    lane = lanes_of(v.shape) % HEAD
    return jnp.where(lane < HEAD // 2, pltpu.roll(v, 96, 1), pltpu.roll(v, 32, 1))


def other_head(v):
    return pltpu.roll(v, HEAD, 1)


def head_means(v):
    low = lanes_of(v.shape) < HEAD
    first = jnp.sum(jnp.where(low, v, 0.0), axis=-1, keepdims=True)
    second = jnp.sum(jnp.where(low, 0.0, v), axis=-1, keepdims=True)
    return jnp.where(low, first, second) * (1.0 / HEAD)


def unit_of(v):
    inverse = lax.rsqrt(jnp.mean(v * v, axis=-1, keepdims=True) + EPSILON)
    return v * inverse, inverse


def norm_back(grad, unit, inverse, gain):
    grad_unit = grad * gain
    return inverse * (grad_unit - unit * jnp.mean(grad_unit * unit, axis=-1, keepdims=True))


def heads_unit(raw):
    inverse = lax.rsqrt(head_means(raw * raw) + EPSILON)
    return raw * inverse, inverse


def heads_back(grad, unit, inverse, gain):
    grad_unit = grad * gain
    return inverse * (grad_unit - unit * head_means(grad_unit * unit))


def rotated(v, cosine, sine):
    return v * cosine + halves_swapped(v) * sine


def rotated_back(v, cosine, sine):
    return v * cosine - halves_swapped(v) * sine


def call(kernel, operands, outs, scratch=(), far=(), small=(), small_outs=(), limit=4, us=1):
    def spec(i, scalars):
        if i in scalars:
            return pl.BlockSpec(memory_space=pltpu.SMEM)
        return pl.BlockSpec(memory_space=pltpu.VMEM)

    in_specs = [
        pl.BlockSpec(memory_space=pl.ANY) if i in far else spec(i, small)
        for i in range(len(operands))
    ]
    return pl.pallas_call(
        kernel,
        out_shape=[jax.ShapeDtypeStruct(shape, kind) for shape, kind in outs],
        in_specs=in_specs,
        out_specs=[spec(i, small_outs) for i in range(len(outs))],
        scratch_shapes=list(scratch),
        compiler_params=pltpu.CompilerParams(vmem_limit_bytes=limit * 1024 * 1024),
        cost_estimate=pl.CostEstimate(
            flops=us * 10**9, bytes_accessed=us * 10**6, transcendentals=0
        ),
    )(*operands)


def fetch(pairs, sems):
    copies = [pltpu.make_async_copy(a, b, sems.at[i]) for i, (a, b) in enumerate(pairs)]
    for copy in copies:
        copy.start()
    return copies


def wait(copies):
    for copy in copies:
        copy.wait()


def repeat(count, body):
    def step(i, carry):
        body(i)
        return carry

    lax.fori_loop(0, count, step, 0)


def rows_at(i, size):
    return pl.ds(pl.multiple_of(i * size, size), size)


def row_of(ref):
    return ref[...].astype(F32).reshape(1, -1)


def place_tables(rows):
    base = (lax.axis_index("dp") % X_SIZE) * rows
    lane = lanes_of((rows // 8, 128))
    rate = jnp.exp((lane % (HEAD // 2)).astype(F32) * (-2.0 / HEAD * math.log(ROPE_BASE)))
    far = (base + 8 * rows_of(lane.shape)).astype(F32) * rate
    near = rows_of((8, 128)).astype(F32) * rate[:8]
    far_c, far_s = jnp.cos(far)[:, None, :], jnp.sin(far)[:, None, :]
    near_c, near_s = jnp.cos(near)[None], jnp.sin(near)[None]
    cosine = (far_c * near_c - far_s * near_s).reshape(rows, 128)
    sine = (far_s * near_c + far_c * near_s).reshape(rows, 128)
    return cosine, jnp.where(lanes_of(sine.shape) % HEAD < HEAD // 2, -sine, sine)


def norm_kv_kernel(tok, gain, wk, wv, kg, normed, packed, raw, cosine, sine):
    rows = tok.shape[0]
    g = row_of(gain)
    for start in range(0, rows, TILE):
        part = pl.ds(start, TILE)
        unit, _ = unit_of(tok[part, :].astype(F32))
        normed[part, :] = (unit * g).astype(BF16)
    weight = jnp.concatenate([wk[...], wv[...]], axis=0)
    kv = dot(normed[...], weight, NT)
    raw[...] = kv
    cosine[...], sine[...] = place_tables(rows)
    unit, _ = heads_unit(kv)
    keys = rotated(unit * two_heads(kg), cosine[...], sine[...])
    packed[...] = jnp.where(lanes_of(kv.shape) < HEAD, keys, kv).astype(BF16)


def two_heads(gain):
    return jnp.concatenate([row_of(gain), row_of(gain)], axis=1)


def query_kernel(
    seg, normed, wq, qg, cosine, sine, cot, wd, meta, low, raw, grad_active, cot_share
):
    q = dot(normed[...], wq[...])
    raw[...] = q
    unit, _ = heads_unit(q)
    low[...] = rotated(unit * two_heads(qg), cosine[...], sine[...]).astype(BF16)
    grad_active[...] = dot(cot[...], wd[...], NT)
    dp, t = lax.axis_index("dp"), lax.axis_index("tensor")
    cot_share[...] = cot[pl.ds(pl.multiple_of(t * 64, 64), 64), :]
    lines = SEQ_LEN // 128
    sequence = seg[pl.ds(pl.multiple_of(dp // X_SIZE * lines, lines), lines), :]
    meta[0] = dp % X_SIZE
    meta[1] = t // 2
    meta[2] = t % 2
    meta[3] = jnp.sum((sequence == jnp.min(sequence)).astype(jnp.int32))
    meta[4] = SEQ_LEN - jnp.sum((sequence == jnp.max(sequence)).astype(jnp.int32))
    meta[5] = dp // X_SIZE
    meta[6] = 0
    meta[7] = 0


def document(place, meta):
    return (place >= meta[3]).astype(jnp.int32) + (place >= meta[4]).astype(jnp.int32)


def key_columns(packed, start, meta):
    shape = packed.shape
    lane = lanes_of(shape)
    mark = jnp.where(lane - HEAD == document(start + rows_of(shape), meta), APART, 0.0)
    return jnp.where(lane < HEAD, packed, mark.astype(BF16))


def value_columns(packed):
    lane = lanes_of(packed.shape)
    return jnp.where(
        lane < HEAD, other_head(packed.astype(F32)), jnp.where(lane < HEAD + 2, 1.0, 0.0)
    ).astype(BF16)


def query_columns(low, start, meta):
    shape = low.shape
    lane = lanes_of(shape)
    wide = low.astype(F32) * (HEAD**-0.5)
    mark = jnp.where(
        (lane - HEAD == document(start + rows_of(shape), meta)) | (lane >= HEAD + 3), 0.0, -APART
    )
    return jnp.concatenate(
        [jnp.where(lane < HEAD, wide, mark), jnp.where(lane < HEAD, other_head(wide), mark)], axis=0
    ).astype(BF16)


def reaches(meta, back, start):
    first_key = (meta[0] - back) * 512
    last_document = document(first_key + 511, meta)
    return (meta[0] >= back) & (last_document >= document(meta[0] * 512 + start, meta))


def attend_kernel(
    meta, low, own, one, two, three, att, output, inverse, key_s, value_s, arrived, sems
):
    rows = low.shape[0]
    copies = fetch([(ref, arrived.at[i]) for i, ref in enumerate((one, two, three))], sems)
    wait(copies)
    pieces = (own, *(arrived.at[i] for i in range(3)))
    for back, piece in enumerate(pieces):

        @pl.when(meta[0] >= back)
        def _(back=back, piece=piece):
            span = pl.ds(back * rows, rows)
            key_s[span, :] = key_columns(piece[...], (meta[0] - back) * rows, meta)
            value_s[span, :] = value_columns(piece[...])

    for start in range(0, rows, TILE):
        reached = pieces_reached(meta, start)
        for count in range(X_SIZE):

            @pl.when(reached == count)
            def _(start=start, count=count):
                part = pl.ds(start, TILE)
                queries = query_columns(low[part, :], meta[0] * rows + start, meta)

                def weighted(first, size, causal):
                    span = pl.ds(first, size)
                    weights = jnp.exp(dot(queries, key_s[span, :], NT))
                    if causal:
                        place = rows_of(weights.shape) % TILE
                        weights = jnp.where(lanes_of(weights.shape) <= place, weights, 0.0)
                    return dot(weights.astype(BF16), value_s[span, :])

                total = weighted(start, TILE, True)
                if start:
                    total = total + weighted(0, start, False)
                if count:
                    total = total + weighted(rows, count * rows, False)
                inverse_total = 1.0 / total[:, HEAD : HEAD + 1]
                result = total * inverse_total
                lane = lanes_of((TILE, 2 * HEAD))
                both = jnp.where(lane < HEAD, result[:TILE], other_head(result[TILE:]))
                att[part, :] = both.astype(BF16)
                output[part, :] = both
                inverse[part, :] = jnp.where(
                    lane < HEAD, inverse_total[:TILE], inverse_total[TILE:]
                )


def pieces_reached(meta, start):
    return sum(reaches(meta, back, start).astype(jnp.int32) for back in range(1, X_SIZE))


def owner(meta, k, c):
    return ((meta[1] + k) % Y_SIZE) * 2 + (meta[2] + c) % 2


def ffn_kernel(meta, *refs):
    att, outw = refs[:8], refs[8:16]
    tok, gain, wg, wu, grad_active = refs[16:21]
    hidden_share, normed, active, grads, keep, give = refs[21:27]
    hidden_s, partial_s, heads_s, weight_s, sems = refs[27:]
    rows, units = grad_active.shape
    pairs = [(w, weight_s.at[pl.ds(i * 128, 128), :]) for i, w in enumerate(outw)]
    for i, a in enumerate(att):
        pairs.append((a, heads_s.at[:, pl.ds(i * 128, 128)]))
    wait(fetch(pairs, sems))
    g = row_of(gain)
    step = 256
    for start in range(0, rows, step):
        part = pl.ds(start, step)
        hidden = tok[part, :].astype(F32) + dot(heads_s[part, :], weight_s[...])
        hidden_s[part, :] = hidden
        unit, _ = unit_of(hidden)
        low = (unit * g).astype(BF16)
        normed[part, :] = low
        gate = dot(low, wg[...], NT)
        upward = dot(low, wu[...], NT)
        sig = jax.nn.sigmoid(gate)
        silu = gate * sig
        active[part, :] = (silu * upward).astype(BF16)
        back = grad_active[part, :]
        grad_gate = (back * upward * sig * (1.0 + gate * (1.0 - sig))).astype(BF16)
        grad_up = (back * silu).astype(BF16)
        grads[part, :] = jnp.concatenate([grad_gate, grad_up], axis=1)
        partial = dot(grad_gate, wg[...]) + dot(grad_up, wu[...])
        partial_s[part, :] = partial.astype(BF16)
    hidden_share[...] = hidden_s[pl.ds(pl.multiple_of(owner(meta, 0, 0) * 64, 64), 64), :]
    split_rows(meta, partial_s, keep, give)


def split_rows(meta, whole, keep, give):
    for k in range(Y_SIZE):
        for c, out in ((0, keep), (1, give)):
            start = pl.multiple_of(owner(meta, k, c) * 64, 64)
            out[k, pl.ds(0, 64), :] = whole[pl.ds(start, 64), :]


def ffn_weights_kernel(meta, normed, grads, cot, active, wd, keys, *refs):
    outs, (far_up, far_down, keep, give, turned), (chunk, terms_s) = refs[:3], refs[3:8], refs[8:]
    for start in range(0, keys.shape[0], 128):
        part = pl.ds(start, 128)
        turned[:, part] = keys[part, :].astype(F32).T.astype(BF16)
    wide, units = grads.shape[1], active.shape[1]
    step = chunk.shape[0]
    for k, out in enumerate((outs[0], outs[1], chunk, outs[2])):
        z = (meta[5] + k) % Z_SIZE
        part = pl.ds(pl.multiple_of(z * step, step), step)
        out[:, pl.ds(0, wide)] = dot(normed[:, part], grads[...], TN).astype(BF16)
        out[:, pl.ds(wide, units)] = dot(cot[:, part], active[...], TN).astype(BF16)
        rest = out.shape[1] - wide - units
        out[:, pl.ds(wide + units, rest)] = jnp.zeros((step, rest), BF16)
    half = far_up.shape[1]
    far_up[...] = chunk[:, pl.ds(0, half)]
    far_down[...] = chunk[:, pl.ds(half, half)]
    terms_s[...] = dot(active[...], wd[...]).astype(BF16)
    split_rows(meta, terms_s, keep, give)


def relay_kernel(near_up, near_down, far_up, far_down, up, down, after, got, sems):
    after[...] = jnp.zeros_like(after)
    copies = fetch([(far_up, got.at[0]), (far_down, got.at[1])], sems)
    half = far_up.shape[1]
    lower, upper = pl.ds(0, half), pl.ds(half, half)
    up[:, upper] = near_up[:, upper]
    down[:, lower] = near_down[:, lower]
    wait(copies)
    for start in range(0, up.shape[0], 64):
        part = pl.ds(start, 64)
        up[part, lower] = (near_up[part, lower].astype(F32) + got[0, part, :].astype(F32)).astype(BF16)
        down[part, upper] = (
            near_down[part, upper].astype(F32) + got[1, part, :].astype(F32)
        ).astype(BF16)


def early_sum_kernel(own, one, two, total, after, near, sems):
    after[...] = jnp.zeros_like(after)
    wait(fetch([(one, near.at[0]), (two, near.at[1])], sems))
    for start in range(0, own.shape[0], 64):
        part = pl.ds(start, 64)
        total[part, :] = (
            own[part, :].astype(F32) + near[0, part, :].astype(F32) + near[1, part, :].astype(F32)
        ).astype(BF16)


def middle_kernel(meta, early, own, *refs):
    far, outs, (near, sems) = refs[:3], refs[3:7], refs[7:]
    wait(fetch([(ref, near.at[i]) for i, ref in enumerate(far)], sems))
    wide = early.shape[1]
    for k, out in enumerate(outs):
        x = (meta[0] + k) % X_SIZE
        part = pl.ds(pl.multiple_of(x * 64, 64), 64)
        out[:, pl.ds(0, wide)] = early[part, :]
        total = own[x].astype(F32)
        for i in range(3):
            total = total + near[i, x].astype(F32)
        out[:, pl.ds(wide, own.shape[2])] = total.astype(BF16)


def weights_kernel(
    own, one, two, three, before, gate, upward, down, query, out, key, value, gains, near, sems
):
    wait(fetch([(ref, near.at[i]) for i, ref in enumerate((one, two, three))], sems))
    total = own[...].astype(F32)
    for i in range(3):
        total = total + near[i].astype(F32)
    units = gate.shape[1]
    gate[...] = total[:, :units]
    upward[...] = total[:, units : 2 * units]
    down[...] = total[:, 2 * units : 3 * units]
    start = total.shape[1] - 512
    query[...] = total[:, start : start + 128]
    out[...] = total[:, start + 128 : start + 256]
    key[...] = total[:, start + 256 : start + 320]
    value[...] = total[:, start + 320 : start + 384]
    gains[...] = total[:16, start + 384 :].astype(BF16)


def add_cores_kernel(keep, got, own, one, two, three, got_s, sems):
    wait(fetch([(got, got_s)], sems))
    for k, out in enumerate((own, one, two, three)):
        out[...] = (keep[k].astype(F32) + got_s[k].astype(F32)).astype(out.dtype)


def total_of(own, far, near, sems):
    wait(fetch([(ref, near.at[i]) for i, ref in enumerate(far)], sems))
    return own[...] + near[0].astype(F32) + near[1].astype(F32) + near[2].astype(F32)


def hidden_back_kernel(
    own, one, two, three, hidden, gain, cot, grad_hidden, low, grad_gain, near, sems
):
    grad = total_of(own, (one, two, three), near, sems)
    unit, inverse = unit_of(hidden[...])
    grad_gain[...] = jnp.sum(grad * unit, axis=0, keepdims=True)
    result = cot[...].astype(F32) + norm_back(grad, unit, inverse, row_of(gain))
    grad_hidden[...] = result
    low[...] = result.astype(BF16)


def attend_back_rows(
    meta, start, low, key_s, value_s, output, inverse, grad_att, grad_k, grad_v, grad_q, acc, turned
):
    rows = low.shape[0]
    part = pl.ds(start, TILE)
    queries = query_columns(low[part, :], meta[0] * rows + start, meta)
    plain = jnp.concatenate(
        [low[part, :], other_head(low[part, :].astype(F32)).astype(BF16)], axis=0
    )
    scaled = (grad_att[part, :].astype(F32) * inverse[part, :] * (HEAD**-0.5)).astype(BF16)
    wide = scaled.astype(F32)
    products = wide * output[part, :]
    lane = lanes_of((TILE, 2 * HEAD))
    heads = []
    for head in range(2):
        mine = (lane < HEAD) if head == 0 else (lane >= HEAD)
        delta = -jnp.sum(jnp.where(mine, products, 0.0), axis=-1, keepdims=True)
        high = delta.astype(BF16).astype(F32)
        value = wide if head == 0 else other_head(wide)
        rest = jnp.where(lane == HEAD, high, jnp.where(lane == HEAD + 1, delta - high, 0.0))
        heads.append(jnp.where(lane < HEAD, value, rest))
    grads = jnp.concatenate(heads, axis=0).astype(BF16)

    def block(span, causal):
        keys = key_s[span, :]
        weights = jnp.exp(dot(keys, queries, NT))
        if causal:
            place = lanes_of(weights.shape) % TILE
            weights = jnp.where(rows_of(weights.shape) <= place, weights, 0.0)
        grad_v[span, :] += dot(weights.astype(BF16), grads)
        scores = (weights * dot(value_s[span, :], grads, NT)).astype(BF16)
        grad_k[span, :] += dot(scores, plain)
        return dot(turned[:, span], scores)

    total = block(pl.ds(start, TILE), True)
    if start:
        total = total + block(pl.ds(0, start), False)
    acc[...] = total

    def piece(i):
        acc[...] += block(rows_at(i + 1, rows), False)

    repeat(pieces_reached(meta, start), piece)

    first, second = acc[:, pl.ds(0, TILE)].T, acc[:, pl.ds(TILE, TILE)].T
    grad_q[part, :] = jnp.where(lane < HEAD, first, other_head(second))


def attend_back_kernel(meta, *refs):
    gathered = refs[:8]
    outw, low, key_s, value_s, output, inverse, turned = refs[8:15]
    whole, grad_q, back_own, back_one, back_two, back_three = refs[16:22]
    grad_k, grad_v, grad_att, acc, sems = refs[22:]
    rows = low.shape[0]
    pairs = []
    for i, part in enumerate(gathered):
        start = pl.multiple_of(owner(meta, -(i // 2) % Y_SIZE, i % 2) * 64, 64)
        pairs.append((part, whole.at[pl.ds(start, 64), :]))
    wait(fetch(pairs, sems))
    grad_att[...] = dot(whole[...], outw[...], NT).astype(BF16)
    grad_k[...] = jnp.zeros_like(grad_k)
    grad_v[...] = jnp.zeros_like(grad_v)
    for start in range(0, rows, TILE):
        attend_back_rows(
            meta, start, low, key_s, value_s, output, inverse, grad_att, grad_k, grad_v, grad_q, acc,
            turned,
        )

    for back, out in enumerate((back_own, back_one, back_two, back_three)):
        lane = lanes_of(out.shape)
        span = pl.ds(back * rows, rows)
        values = other_head(grad_v[span, :]) * (HEAD**0.5)
        out[...] = jnp.where(lane < HEAD, grad_k[span, :], values).astype(out.dtype)


def query_back_kernel(
    grad_rot, raw, qg, cosine, sine, normed, whole, att, low, summed, grad_gain
):
    grad = rotated_back(grad_rot[...], cosine[...], sine[...])
    unit, inverse = heads_unit(raw[...])
    gain_both = jnp.sum(grad * unit, axis=0, keepdims=True)
    grad_gain[...] = gain_both + other_head(gain_both)
    low[...] = heads_back(grad, unit, inverse, two_heads(qg)).astype(BF16)
    wide = low.shape[1]
    summed[:, :, pl.ds(0, wide)] = dot(normed[...], low[...], TN).astype(BF16).reshape(16, 64, wide)
    summed[:, :, pl.ds(wide, wide)] = (
        dot(whole[...], att[...], TN).astype(BF16).reshape(16, 64, wide)
    )


def key_back_kernel(
    meta, own, one, two, three, raw, kg, cosine, sine, normed, grad_q, wq, wk, wv, tok,
    ffn_gain, q_gain, before, keep_terms, give_terms, before_this, first, second, third, fourth, keep, give, summed, partial_s, low_s, near, sems,
):
    lane = lanes_of(own.shape)
    rot = total_of(own, (one, two, three), near, sems)
    grad = rotated_back(rot, cosine[...], sine[...])
    unit, inverse = heads_unit(raw[...])
    k_gain = jnp.sum(jnp.where(lane < HEAD, grad * unit, 0.0), axis=0, keepdims=True)
    keys = heads_back(grad, unit, inverse, two_heads(kg))
    low = jnp.where(lane < HEAD, keys, rot).astype(BF16)
    wide = low.shape[1]
    summed[:, :, pl.ds(0, 2 * wide)] = before[...]
    summed[:, :, pl.ds(2 * wide, wide)] = (
        dot(normed[...], low, TN).astype(BF16).reshape(16, 64, wide)
    )
    kv_weight = jnp.concatenate([wk[...], wv[...]], axis=0)
    low_s[...] = low

    def block(i, a_gain):
        part = rows_at(i, 256)
        partial = dot(grad_q[part, :], wq[...], NT) + dot(low_s[part, :], kv_weight)
        partial_s[part, :] = partial.astype(BF16)
        token_unit, _ = unit_of(tok[part, :].astype(F32))
        return a_gain + jnp.sum(partial * token_unit, axis=0, keepdims=True)

    a_gain = lax.fori_loop(0, own.shape[0] // 256, block, jnp.zeros((1, tok.shape[1]), F32))
    split_rows(meta, partial_s, keep, give)
    for k in range(Y_SIZE):
        keep[k, pl.ds(64, 64), :] = keep_terms[k]
        give[k, pl.ds(64, 64), :] = give_terms[k]
    summed[:, :, pl.ds(3 * wide, wide)] = jnp.zeros((16, 64, wide), BF16)
    half, rest = jnp.zeros((1, 64), F32), jnp.zeros((12, 128), F32)
    for p in range(16):
        own_rows = [
            jnp.concatenate([gain[:, p * 64 : (p + 1) * 64], half], axis=1)
            for gain in (a_gain, ffn_gain[...])
        ]
        lines = jnp.concatenate([*own_rows, q_gain[...], k_gain, rest], axis=0)
        summed[p, pl.ds(0, 16), pl.ds(3 * wide, wide)] = lines.astype(BF16)
    for k, out in enumerate((first, second, third, fourth)):
        out[...] = summed[pl.ds((meta[5] + k) % Z_SIZE * X_SIZE, X_SIZE)]


def final_kernel(
    meta, own, one, two, three, tok, gain, grad_hidden, hidden, grad_tokens, result, after, near, sems
):
    after[...] = jnp.zeros_like(after)
    total = total_of(own, (one, two, three), near, sems)
    mine = tok[pl.ds(pl.multiple_of(owner(meta, 0, 0) * 64, 64), 64), :].astype(F32)
    unit, inverse = unit_of(mine)
    grad_tokens[...] = grad_hidden[...] + norm_back(total[:64], unit, inverse, row_of(gain))
    result[...] = (hidden[...] + total[64:]).astype(BF16)


def gains_kernel(*refs):
    parts, (attn, ffn, query, key) = refs[:8], refs[8:]
    total = 0.0
    for part in parts:
        total = total + part[...].astype(F32)
    attn[...] = total[0:1, :64]
    ffn[...] = total[1:2, :64]
    mine = pltpu.roll(total, 128 - lax.axis_index("dp") * 4, 1)
    query[...] = mine[2:3, :4]
    key[...] = mine[3:4, :4]


def sems(count):
    return pltpu.SemaphoreType.DMA((count,))


def sum_at_owner(keep, give):
    got = over_cores(give)
    shape = keep.shape[1:]
    own, one, two, three = call(
        add_cores_kernel,
        [keep, got],
        [(shape, F32)] + [(shape, BF16)] * 3,
        scratch=[pltpu.VMEM(got.shape, BF16), sems(1)],
        far=(1,),
    )
    return own, along_y(one, 1), along_y(two, 2), along_y(three, 3)


def local(
    tokens, segments, attn_gain, query_weight, key_weight, value_weight, query_gain, key_gain,
    out_weight, ffn_gain, gate_weight, up_weight, down_weight, cotangent,
):
    rows, width = tokens.shape
    units = gate_weight.shape[1]
    early_wide = -(-3 * units // 128) * 128
    key_weight, value_weight = key_weight.T, value_weight.T
    gate_weight, up_weight = gate_weight.T, up_weight.T
    normed, packed, kv_raw, cosine, sine = call(
        norm_kv_kernel,
        [tokens, attn_gain, key_weight, value_weight, key_gain],
        [((rows, width), BF16), ((rows, 128), BF16)] + [((rows, 128), F32)] * 3,
    )
    arrived = [in_sequence(packed, k) for k in range(1, X_SIZE)]
    out_here = lax.optimization_barrier((packed, out_weight))[1]
    meta, q_low, q_raw, grad_active, cot_share = call(
        query_kernel,
        [
            segments.reshape(-1, 128), normed, query_weight, query_gain, cosine, sine, cotangent,
            down_weight,
        ],
        [
            ((8,), jnp.int32), ((rows, 128), BF16), ((rows, 128), F32), ((rows, units), F32),
            ((64, width), BF16),
        ],
        small_outs=(0,),
        us=2,
    )
    att, output, inverse, keys, values = call(
        attend_kernel,
        [meta, q_low, packed, *arrived],
        [((rows, 128), BF16), ((rows, 128), F32), ((rows, 128), F32)]
        + [((X_SIZE * rows, 128), BF16)] * 2,
        scratch=[
            pltpu.VMEM((X_SIZE - 1, rows, 128), BF16),
            sems(3),
        ],
        small=(0,),
        far=(3, 4, 5),
        us=6,
    )
    out_all = gather_relative(out_here)
    att_all = gather_relative(att)
    hidden_share, normed_two, active, grads, keep, give = call(
        ffn_kernel,
        [meta, *att_all, *out_all, tokens, ffn_gain, gate_weight, up_weight, grad_active],
        [
            ((64, width), F32), ((rows, width), BF16), ((rows, units), BF16),
            ((rows, 2 * units), BF16), ((Y_SIZE, 64, width), BF16), ((Y_SIZE, 64, width), BF16),
        ],
        scratch=[
            pltpu.VMEM((rows, width), F32),
            pltpu.VMEM((rows, width), BF16),
            pltpu.VMEM((rows, width), BF16),
            pltpu.VMEM((width, width), BF16),
            sems(16),
        ],
        small=(0,),
        far=tuple(range(1, 17)),
        limit=12,
        us=7,
    )
    shares = sum_at_owner(keep, give)
    *early_parts, keep_terms, give_terms, keys_turned = call(
        ffn_weights_kernel,
        [meta, normed_two, grads, cotangent, active, down_weight, keys],
        [((256, early_wide), BF16)] * 3
        + [((256, early_wide // 2), BF16)] * 2
        + [((Y_SIZE, 64, width), BF16)] * 2
        + [((128, X_SIZE * rows), BF16)],
        scratch=[pltpu.VMEM((256, early_wide), BF16), pltpu.VMEM((rows, width), BF16)],
        small=(0,),
        limit=8,
        us=4,
    )
    shares = lax.optimization_barrier((*shares, *early_parts))
    shares, early_parts = shares[:4], shares[4:]
    share = pltpu.VMEM((X_SIZE - 1, 64, width), BF16)
    grad_hidden, grad_hidden_low, grad_ffn_gain = call(
        hidden_back_kernel,
        [*shares, hidden_share, ffn_gain, cot_share],
        [((64, width), F32), ((64, width), BF16), ((1, width), F32)],
        scratch=[share, sems(3)],
        far=(1, 2, 3),
    )
    gathered = gather_relative(grad_hidden_low)
    own_chunk, near_up, near_down, far_up, far_down = early_parts
    up, down, relay_done = call(
        relay_kernel,
        [near_up, near_down, along_z(far_up, 1), along_z(far_down, -1)],
        [((256, early_wide), BF16)] * 2 + [((8, 128), F32)],
        scratch=[pltpu.VMEM((2, 256, early_wide // 2), BF16), sems(2)],
        far=(2, 3),
    )
    early = [own_chunk, along_z(up, 1), along_z(down, -1)]
    whole, grad_q_rot, back_own, *backs = call(
        attend_back_kernel,
        [
            meta, *gathered, out_weight, q_low, keys, values, output, inverse, keys_turned,
            relay_done,
        ],
        [((rows, width), BF16), ((rows, 128), F32), ((rows, 128), F32)]
        + [((rows, 128), BF16)] * 3,
        scratch=[
            pltpu.VMEM((X_SIZE * rows, 128), F32),
            pltpu.VMEM((X_SIZE * rows, 128), F32),
            pltpu.VMEM((rows, 128), BF16),
            pltpu.VMEM((128, 2 * TILE), F32),
            sems(8),
        ],
        small=(0,),
        far=tuple(range(1, 9)),
        limit=12,
        us=8,
    )
    returned = [in_sequence(value, -k - 1) for k, value in enumerate(backs)]
    grad_q_low, late_first, grad_q_gain = call(
        query_back_kernel,
        [grad_q_rot, q_raw, query_gain, cosine, sine, normed, whole, att],
        [((rows, 128), BF16), ((16, 64, 256), BF16), ((1, 128), F32)],
    )
    early_sum, early_done = call(
        early_sum_kernel,
        early,
        [((256, early_wide), BF16), ((8, 128), F32)],
        scratch=[pltpu.VMEM((2, 256, early_wide), BF16), sems(2)],
        far=(1, 2),
    )
    *late_parts, keep, give = call(
        key_back_kernel,
        [
            meta, back_own, *returned, kv_raw, key_gain, cosine, sine, normed, grad_q_low,
            query_weight, key_weight, value_weight, tokens, grad_ffn_gain, grad_q_gain, late_first,
            keep_terms, give_terms, early_done,
        ],
        [((X_SIZE, 64, 512), BF16)] * 4 + [((Y_SIZE, 128, width), BF16)] * 2,
        scratch=[
            pltpu.VMEM((16, 64, 512), BF16),
            pltpu.VMEM((rows, width), BF16),
            pltpu.VMEM((rows, 128), BF16),
            pltpu.VMEM((X_SIZE - 1, rows, 128), BF16),
            sems(3),
        ],
        small=(0,),
        far=(2, 3, 4),
        limit=10,
        us=3,
    )
    late = sent_on(late_parts, along_z)
    grad_tokens, block_output, rows_done = call(
        final_kernel,
        [meta, *sum_at_owner(keep, give), tokens, attn_gain, grad_hidden, hidden_share],
        [((64, width), F32), ((64, width), BF16), ((8, 128), F32)],
        scratch=[pltpu.VMEM((X_SIZE - 1, 128, width), BF16), sems(3)],
        small=(0,),
        far=(2, 3, 4),
    )
    all_wide = early_wide + 512
    parts = sent_on(
        call(
            middle_kernel,
            [meta, early_sum, *late],
            [((64, all_wide), BF16)] * 4,
            scratch=[
                pltpu.VMEM((3, X_SIZE, 64, 512), BF16),
                sems(3),
            ],
            small=(0,),
            far=(3, 4, 5),
        ),
        along_x,
    )
    gate_grad, up_grad, down_grad, query_grad, out_grad, key_grad, value_grad, gain_parts = call(
        weights_kernel,
        [*parts, rows_done],
        [((64, units), F32)] * 3
        + [((64, 128), F32), ((64, 128), F32), ((64, 64), F32), ((64, 64), F32), ((16, 128), BF16)],
        scratch=[pltpu.VMEM((3, 64, all_wide), BF16), sems(3)],
        far=(1, 2, 3),
    )
    gains = call(
        gains_kernel,
        gather_relative(gain_parts),
        [((1, 64), F32), ((1, 64), F32), ((1, 4), F32), ((1, 4), F32)],
    )
    return (
        block_output, grad_tokens, gains[0].reshape(-1), query_grad, key_grad, value_grad,
        gains[2].reshape(-1), gains[3].reshape(-1), out_grad.T, gains[1].reshape(-1), gate_grad,
        up_grad, down_grad.T,
    )


def solution(mesh):
    rows_split, columns_split, copied = P("dp", None), P(None, "tensor"), P()
    in_specs = (
        rows_split, copied, copied, columns_split, columns_split, columns_split, copied, copied,
        P("tensor", None), copied, columns_split, columns_split, P("tensor", None), rows_split,
    )
    both, across = P(("dp", "tensor"), None), P("dp", "tensor")
    out_specs = (
        both, both, P("dp"), across, across, across, P("dp"), P("dp"), P("tensor", "dp"), P("dp"),
        across, across, P("tensor", "dp"),
    )
    return jax.shard_map(local, mesh=mesh, in_specs=in_specs, out_specs=out_specs, check_vma=False)
```
